128 devices in a mesh: grp: 16 (over x_hi, y, core), mem: 8 (over x_lo, z).
Axes of the slice: x: 4 (x_hi: 2, x_lo: 2; x = x_hi * 2 + x_lo), y: 4, z: 4, core: 2. Of those that a mesh axis runs over, the one named last changes fastest.
Arguments:
- q_branch: bfloat16 [16384, 4096], P(('grp', 'mem')), parts along dimension 0, may hold values from -6 to 6
- k_branch: bfloat16 [16384, 512], P(('grp', 'mem')), parts along dimension 0, may hold values from -6 to 6
- v_branch: bfloat16 [16384, 512], P(('grp', 'mem')), parts along dimension 0, may hold values from -6 to 6
- k_root: bfloat16 [32768, 512], P(('grp', 'mem')), parts along dimension 0, may hold values from -6 to 6
- v_root: bfloat16 [32768, 512], P(('grp', 'mem')), parts along dimension 0, may hold values from -6 to 6
- d_out: bfloat16 [16384, 4096], P(('grp', 'mem')), parts along dimension 0, may hold values from -6 to 6
- lengths: int32 [128, 4], P(('grp', 'mem')), parts along dimension 0, may hold values from 1 to 64, 128 in all within a row
- forks: int32 [128, 4], P(('grp', 'mem')), parts along dimension 0, may hold values from 2 to 2048
Outputs:
- dq_branch: bfloat16 [16384, 4096], P(('grp', 'mem')), parts along dimension 0
- dk_branch: bfloat16 [16384, 512], P(('grp', 'mem')), parts along dimension 0
- dv_branch: bfloat16 [16384, 512], P(('grp', 'mem')), parts along dimension 0
- dk_root: bfloat16 [32768, 512], P(('grp', 'mem')), parts along dimension 0
- dv_root: bfloat16 [32768, 512], P(('grp', 'mem')), parts along dimension 0
The draws below stay inside these ranges and needn't reach their ends.
There are 16 independent parts, one for each index of `grp`. The reference program is written for one: setup_inputs(seed, part) draws one part's arguments, and reference() takes and returns one part's arrays. A program takes and returns all parts, laid end to end along the dimension named above; each array names one. Nothing has to cross between parts.
Inputs may be any that keep to these rules, and one draw needn't show every extreme that they name: Each row's 4 lengths sum to 128.
All inputs are finite; a program needn't handle non-finite values.
Results may differ from the reference program's by a relative error of at most 0.02.
Values may be sent and summed in bfloat16 or wider, within the bound.
A program may use at most 128 MiB of HBM per device.

```python
import math
import jax
import jax.numpy as jnp
import numpy as np
from jax import lax

H = 32
KVH = 4
HD = 128
BR_DEV = 128
NB = 4
ROOT = 2048
BRANCH = 1024
N_MEM = 8


def draw_q_branch(key, part):
    key = jax.random.fold_in(key, 11)
    values_drawn = jax.random.truncated_normal(key, -6.0, 6.0, (BRANCH, H, HD), jnp.float32)
    return values_drawn.reshape(BRANCH, H * HD).astype(jnp.bfloat16)


def draw_k_root(key, part):
    key = jax.random.fold_in(key, 23)
    values_drawn = jax.random.truncated_normal(key, -6.0, 6.0, (ROOT, KVH, HD), jnp.float32)
    return values_drawn.reshape(ROOT, KVH * HD).astype(jnp.bfloat16)


def plant(array, own_key, least, top_value):
    shape = array.shape
    place = [jax.random.randint(jax.random.fold_in(own_key, axis), (), 0, shape[axis]) for axis in range(len(shape))]
    array = array.at[tuple(place)].set(least)
    longest = shape.index(max(shape))
    place[longest] = (place[longest] + 1) % shape[longest]
    return array.at[tuple(place)].set(top_value)


def steps_of(own_key, dims, shards, smallest, largest):
    level, own = 1.0, jax.random.fold_in(own_key, 6)
    for position, blocks in shards:
        heights = jnp.exp(jax.random.uniform(jax.random.fold_in(own, position), (blocks,), jnp.float32, smallest / len(shards), largest / len(shards)))
        level = level * jnp.repeat(heights, dims[position] // blocks).reshape([-1 if axis == position else 1 for axis in range(len(dims))])
    return level


def profile(count, total, bound, slope):
    portions = [(1 << 20) // math.isqrt(rank ** slope) + 1 for rank in range(2, count + 1)]
    surplus, counts = total - bound - (count - 1), [1] * (count - 1)
    while surplus > 0:
        candidates = [i for i in range(count - 1) if counts[i] < bound]
        whole, budget = sum([portions[i] for i in candidates]), surplus
        for i in candidates:
            more = min(bound - counts[i], max(1, budget * portions[i] // whole), surplus)
            counts[i] = counts[i] + more
            surplus = surplus - more
    return np.array([bound] + counts)


def uneven_parts(key, number_of, total, reach, skew):
    if number_of == 2:
        one = jax.random.randint(key, (), max(1, total - reach), min(reach, total - 1) + 1)
        return jnp.stack([one, total - one])
    tallies = jnp.asarray(profile(number_of, total, reach, skew), jnp.int32)
    twos = (number_of - 1) // 2
    donor, sink = tallies[1:1 + 2 * twos:2], tallies[2:2 + 2 * twos:2]
    margin = jnp.minimum(donor - 1, reach - sink)
    moved = jax.random.randint(jax.random.fold_in(key, 1), (twos,), 0, 1 << 20) % (margin + 1)
    tallies = tallies.at[1:1 + 2 * twos:2].set(donor - moved).at[2:2 + 2 * twos:2].set(sink + moved)
    return tallies[jax.random.permutation(jax.random.fold_in(key, 2), number_of)]


def noise(own_key, shape, spread, bound, shards=(), kind=jnp.bfloat16):
    gain = steps_of(own_key, shape, shards, -0.22, 0.18) if shards else 1.0
    drawn = jax.random.normal(own_key, shape, jnp.float32) * spread * gain
    return jnp.minimum(jnp.maximum(drawn, -bound), bound).astype(kind)


def setup_inputs(seed: int = 0, part: int = 0) -> dict:
    key_of = jax.random.split(jax.random.key(seed), 9)
    part_splits = jax.random.split(jax.random.fold_in(key_of[8], part), 9)
    return {
        "q_branch": draw_q_branch(jax.random.fold_in(jax.random.fold_in(key_of[8], part), 71), part),
        "k_branch": noise(part_splits[1], (BRANCH, KVH * HD), 1.0, 6.0, ((0, 8),)),
        "v_branch": noise(part_splits[2], (BRANCH, KVH * HD), 1.0, 6.0, ((0, 8),)),
        "k_root": draw_k_root(jax.random.fold_in(jax.random.fold_in(key_of[8], part), 71), part),
        "v_root": noise(part_splits[4], (ROOT, KVH * HD), 1.0, 6.0, ((0, 8),)),
        "d_out": noise(part_splits[5], (BRANCH, H * HD), 1.0, 6.0, ((0, 8),)),
        "lengths": jax.vmap(lambda own: uneven_parts(own, NB, BR_DEV, BR_DEV // 2, 2))(jax.random.split(part_splits[6], N_MEM)).reshape((N_MEM, NB)).astype(jnp.int32),
        "forks": plant(jax.random.randint(part_splits[7], (N_MEM, NB), 2, ROOT + 1), jax.random.fold_in(part_splits[7], 1), 2, ROOT).astype(jnp.int32),
    }


def reference(q_branch, k_branch, v_branch, k_root, v_root, d_out, lengths, forks):
    group_size = H // KVH
    score_scale = 1.0 / math.sqrt(HD)
    kv_width = KVH * HD
    keys_root = k_root.astype(jnp.float32).reshape(ROOT, KVH, HD)
    values_root = v_root.astype(jnp.float32).reshape(ROOT, KVH, HD)

    def device_step(running, device_index):
        acc_keys, acc_values = running
        first_row = (device_index * BR_DEV).astype(jnp.int32)
        queries = lax.dynamic_slice_in_dim(q_branch, first_row, BR_DEV, 0).astype(jnp.float32).reshape(BR_DEV, KVH, group_size, HD)
        grad_out = lax.dynamic_slice_in_dim(d_out, first_row, BR_DEV, 0).astype(jnp.float32).reshape(BR_DEV, KVH, group_size, HD)
        own_keys = lax.dynamic_slice_in_dim(k_branch, first_row, BR_DEV, 0).astype(jnp.float32).reshape(BR_DEV, KVH, HD)
        own_values = lax.dynamic_slice_in_dim(v_branch, first_row, BR_DEV, 0).astype(jnp.float32).reshape(BR_DEV, KVH, HD)
        branch_lens = lax.dynamic_slice_in_dim(lengths, device_index.astype(jnp.int32), 1, 0)[0]
        fork_points = lax.dynamic_slice_in_dim(forks, device_index.astype(jnp.int32), 1, 0)[0]
        branch_ends = jnp.cumsum(branch_lens)
        places = jnp.arange(BR_DEV, dtype=jnp.int32)
        segment = lax.optimization_barrier(jnp.sum((places[:, None] >= branch_ends[None, :]).astype(jnp.int32), axis=1))
        fork_row = fork_points[segment]
        root_seen = jnp.arange(ROOT, dtype=jnp.int32)[None, :] < fork_row[:, None]
        own_seen = (segment[:, None] == segment[None, :]) & (places[None, :] <= places[:, None])
        visible = jnp.concatenate([root_seen, own_seen], axis=1)[:, None, None, :]
        all_keys = jnp.concatenate([keys_root, own_keys], axis=0)
        all_values = jnp.concatenate([values_root, own_values], axis=0)
        scores = jnp.einsum('rkgd,nkd->rkgn', queries, all_keys) * score_scale
        masked = jnp.where(visible, scores, -jnp.inf)
        row_max = lax.optimization_barrier(jnp.max(masked, axis=-1, keepdims=True))
        log_norm = row_max + jnp.log(lax.optimization_barrier(jnp.sum(jnp.exp(masked - row_max), axis=-1, keepdims=True)))
        weights = jnp.where(visible, jnp.exp(scores - log_norm), 0.0)
        weights_low = lax.optimization_barrier(weights.astype(jnp.bfloat16)).astype(jnp.float32)
        attended = jnp.einsum('rkgn,nkd->rkgd', weights_low, all_values)
        correction = lax.optimization_barrier(jnp.sum(grad_out * attended, axis=-1, keepdims=True))
        grad_weights = jnp.einsum('rkgd,nkd->rkgn', grad_out, all_values)
        grad_scores = lax.optimization_barrier((weights * (grad_weights - correction)).astype(jnp.bfloat16)).astype(jnp.float32)
        grad_query = jnp.einsum('rkgn,nkd->rkgd', grad_scores, all_keys) * score_scale
        grad_keys = jnp.einsum('rkgn,rkgd->nkd', grad_scores, queries) * score_scale
        grad_values = jnp.einsum('rkgn,rkgd->nkd', weights_low, grad_out)
        acc_keys = acc_keys + grad_keys[:ROOT].reshape(ROOT, kv_width)
        acc_values = acc_values + grad_values[:ROOT].reshape(ROOT, kv_width)
        results = (grad_query.reshape(BR_DEV, H * HD).astype(jnp.bfloat16), grad_keys[ROOT:].reshape(BR_DEV, kv_width).astype(jnp.bfloat16), grad_values[ROOT:].reshape(BR_DEV, kv_width).astype(jnp.bfloat16))
        return ((acc_keys, acc_values), results)
    start_acc = (jnp.zeros((ROOT, kv_width), jnp.float32), jnp.zeros((ROOT, kv_width), jnp.float32))
    (acc_keys, acc_values), stacked = lax.scan(device_step, start_acc, jnp.arange(N_MEM, dtype=jnp.int32))
    dq_branch = stacked[0].reshape(BRANCH, H * HD)
    dk_branch = stacked[1].reshape(BRANCH, kv_width)
    dv_branch = stacked[2].reshape(BRANCH, kv_width)
    return (dq_branch, dk_branch, dv_branch, acc_keys.astype(jnp.bfloat16), acc_values.astype(jnp.bfloat16))
```

```python
import functools
import math

import jax
import jax.numpy as jnp
from jax import lax
from jax.experimental import pallas as pl
from jax.experimental.pallas import tpu as pltpu
from jax.sharding import PartitionSpec as P

KVH = 4
GROUP = 8
HD = 128
TOK = 128
NQ = GROUP * TOK
SHARD = 256
HALF = SHARD // 2
N_MEM = 8
RING = 4
ROOT = SHARD * N_MEM
LT = 256
NEG = -1e30
SCALE = 1.0 / math.sqrt(HD)
C2 = SCALE / math.log(2.0)
SLOTS = 31
F32 = jnp.float32
BF16 = jnp.bfloat16
NT = (((1,), (1,)), ((), ()))


def kernel(
    q_in, kb_in, vb_in, kr_in, vr_in, do_in, len_in, fork_in,
    dq_out, dkb_out, dvb_out, dkr_out, dvr_out,
    qs, gs, kbuf, vbuf, pk, pv, rk, rkx, rvx, rvh, rvf,
    exp_own, dp_own, exp_all, dp_all, maxes, total, corr, dq_acc, fork_row, start_row,
    ssem, rsem, lsem,
):
    me = lax.axis_index("mem")
    x, z = me // RING, me % RING
    xn = 1 - x
    zp, zm, z2 = (z + 1) % RING, (z + 3) % RING, (z + 2) % RING

    def at(xi, zi):
        return xi * RING + zi

    def rows(xi, zi, first=0, count=SHARD):
        return pl.ds(pl.multiple_of(at(xi, zi) * SHARD + first, HALF), count)

    def head_cols(h):
        return pl.ds(pl.multiple_of(h * HD, HD), HD)

    right, left, across = at(x, zp), at(x, zm), at(xn, z)

    def copy(h, slot):
        own_k, own_v = kr_in.at[:, head_cols(h)], vr_in.at[:, head_cols(h)]

        def kv(buf, xi, zi, first=0, count=SHARD):
            return buf.at[h, rows(xi, zi, first, count), :]

        def same(buf, xi, zi, to, first=0, count=SHARD):
            ref = kv(buf, xi, zi, first, count)
            return ref, ref, to

        src, dst, to = {
            0: lambda: (own_k, kv(kbuf, x, z), across),
            1: lambda: (own_k, kv(kbuf, x, z), right),
            2: lambda: (own_k, kv(kbuf, x, z), left),
            3: lambda: same(kbuf, xn, z, right),
            4: lambda: same(kbuf, xn, z, left),
            5: lambda: same(kbuf, x, zm, right),
            6: lambda: same(kbuf, xn, zp, left),
            7: lambda: (own_v, kv(vbuf, x, z), across),
            8: lambda: (own_v, kv(vbuf, x, z), right),
            9: lambda: (own_v, kv(vbuf, x, z), left),
            10: lambda: same(vbuf, x, zm, right, 0, HALF),
            11: lambda: same(vbuf, x, zp, left, HALF, HALF),
            12: lambda: same(vbuf, x, zm, across),
            13: lambda: same(vbuf, x, zp, across),
            14: lambda: same(vbuf, x, z2, across, 0, HALF),
            15: lambda: same(vbuf, x, z2, across, HALF, HALF),
            16: lambda: (kv(pk, x, z2), rk.at[h, 0], right),
            17: lambda: (kv(pk, xn, z2), rk.at[h, 1], left),
            18: lambda: (kv(pk, xn, zp), rk.at[h, 2], right),
            19: lambda: (kv(pk, x, zm), rk.at[h, 3], left),
            20: lambda: (kv(pk, x, zp), rk.at[h, 4], right),
            21: lambda: (kv(pk, xn, zm), rk.at[h, 5], left),
            22: lambda: (kv(pk, xn, z), rkx.at[h], across),
            23: lambda: (kv(pv, xn, z2), rvx.at[h, 0], across),
            24: lambda: (kv(pv, xn, zp), rvx.at[h, 1], across),
            25: lambda: (kv(pv, xn, zm), rvx.at[h, 2], across),
            26: lambda: (kv(pv, xn, z), rvx.at[h, 3], across),
            27: lambda: (kv(pv, x, z2, 0, HALF), rvh.at[h, 0], right),
            28: lambda: (kv(pv, x, z2, HALF, HALF), rvh.at[h, 1], left),
            29: lambda: (kv(pv, x, zp), rvf.at[h, 0], right),
            30: lambda: (kv(pv, x, zm), rvf.at[h, 1], left),
        }[slot]()
        return pltpu.make_async_remote_copy(
            src_ref=src, dst_ref=dst,
            send_sem=ssem.at[h, slot], recv_sem=rsem.at[h, slot],
            device_id={"mem": to}, device_id_type=pl.DeviceIdType.MESH,
        )

    def send(h, *slots):
        for slot in slots:
            copy(h, slot).start()

    def arrive(h, *slots):
        for slot in slots:
            copy(h, slot).wait_recv()

    def local(h, which):
        src, buf = ((kr_in, kbuf), (vr_in, vbuf))[which]
        return pltpu.make_async_copy(
            src.at[:, head_cols(h)], buf.at[h, rows(x, z), :], lsem.at[h, which]
        )

    def gather0(h):
        send(h, 0, 8, 9, 1, 2, 7)

    def gather1(h):
        arrive(h, 0, 8, 9, 1)
        send(h, 10, 11, 3, 4, 12, 13, 5)

    def gather2(h):
        arrive(h, 10, 11, 4)
        send(h, 14, 15, 6)

    def gather3(h):
        arrive(h, 2, 3, 5, 6, 7, 12, 13, 14, 15)

    def f32(ref):
        return ref.astype(F32)

    def reduce1(h):
        arrive(h, 23)
        here = rows(x, z2)
        pv[h, here, :] = (f32(pv[h, here, :]) + f32(rvx[h, 0])).astype(BF16)
        send(h, 27, 28)
        arrive(h, 16)
        here = rows(x, zp)
        pk[h, here, :] = (f32(pk[h, here, :]) + f32(rk[h, 0])).astype(BF16)
        send(h, 20)
        arrive(h, 17)
        here = rows(xn, zm)
        pk[h, here, :] = (f32(pk[h, here, :]) + f32(rk[h, 1])).astype(BF16)
        send(h, 21)

    def reduce2(h):
        arrive(h, 24, 25, 27, 28)
        here, rest = rows(x, zp, 0, HALF), rows(x, zp, HALF, HALF)
        pv[h, here, :] = (f32(pv[h, here, :]) + f32(rvx[h, 1, :HALF]) + f32(rvh[h, 0])).astype(BF16)
        pv[h, rest, :] = (f32(pv[h, rest, :]) + f32(rvx[h, 1, HALF:])).astype(BF16)
        send(h, 29)
        here, rest = rows(x, zm, HALF, HALF), rows(x, zm, 0, HALF)
        pv[h, here, :] = (f32(pv[h, here, :]) + f32(rvx[h, 2, HALF:]) + f32(rvh[h, 1])).astype(BF16)
        pv[h, rest, :] = (f32(pv[h, rest, :]) + f32(rvx[h, 2, :HALF])).astype(BF16)
        send(h, 30)
        arrive(h, 18, 21)
        here = rows(xn, z)
        pk[h, here, :] = (f32(pk[h, here, :]) + f32(rk[h, 2]) + f32(rk[h, 5])).astype(BF16)
        send(h, 22)

    def reduce3(h):
        own = rows(x, z)
        arrive(h, 26, 29, 30)
        dvr_out[:, head_cols(h)] = (
            f32(pv[h, own, :]) + f32(rvx[h, 3]) + f32(rvf[h, 0]) + f32(rvf[h, 1])
        ).astype(BF16)
        arrive(h, 19, 20, 22)
        dkr_out[:, head_cols(h)] = (
            f32(pk[h, own, :]) + f32(rk[h, 3]) + f32(rk[h, 4]) + f32(rkx[h])
        ).astype(BF16)

    barrier = pltpu.get_barrier_semaphore()
    for peer in (right, left, across):
        pl.semaphore_signal(
            barrier, inc=1, device_id={"mem": peer}, device_id_type=pl.DeviceIdType.MESH
        )
    for h in range(KVH):
        local(h, 0).start()
        local(h, 1).start()
    pl.semaphore_wait(barrier, 3)
    gather0(0)
    gather0(1)

    lens = [len_in[0, b] for b in range(4)]
    ends = [lens[0], lens[0] + lens[1], lens[0] + lens[1] + lens[2]]
    place = lax.broadcasted_iota(jnp.int32, (1, NQ), 1) % TOK
    fork = jnp.full((1, NQ), fork_in[0, 0], jnp.int32)
    start = jnp.zeros((1, NQ), jnp.int32)
    for b, end in enumerate(ends):
        fork = jnp.where(place >= end, fork_in[0, b + 1], fork)
        start = jnp.where(place >= end, end, start)
    fork_row[...] = fork
    start_row[...] = start

    def lay_out(h, carry):
        for g in range(GROUP):
            cols = pl.ds(pl.multiple_of((h * GROUP + g) * HD, HD), HD)
            qs[h, g * TOK : (g + 1) * TOK, :] = q_in[:, cols]
            gs[h, g * TOK : (g + 1) * TOK, :] = do_in[:, cols]
        return carry

    lax.fori_loop(0, KVH, lay_out, 0)
    gather1(0)
    gather2(0)
    for h in range(KVH):
        local(h, 0).wait()
        local(h, 1).wait()

    order = [
        (xn, z2), (x, z2), (xn, zp), (xn, zm), (xn, z), (x, zp), (x, zm), (x, z),
    ]

    def scores(key, h, lanes):
        return lax.dot_general(key, qs[h, lanes, :], NT, preferred_element_type=F32)

    def grads(value, h, lanes):
        return lax.dot_general(value, gs[h, lanes, :], NT, preferred_element_type=F32)

    lane_tiles = [slice(t, t + LT) for t in range(0, NQ, LT)]

    def first_own(h):
        key, value = kb_in[:, head_cols(h)], vb_in[:, head_cols(h)]
        for lanes in lane_tiles:
            row = lax.broadcasted_iota(jnp.int32, (TOK, LT), 0)
            lane = lax.broadcasted_iota(jnp.int32, (TOK, LT), 1) % TOK
            seen = (row <= lane) & (row >= start_row[:, lanes])
            s = jnp.where(seen, scores(key, h, lanes), NEG)
            top = jnp.max(s, axis=0, keepdims=True)
            e = jnp.exp2(s * C2 - top * C2)
            dp = grads(value, h, lanes)
            total[:, lanes] = jnp.sum(e, axis=0, keepdims=True)
            corr[:, lanes] = jnp.sum(e * dp, axis=0, keepdims=True)
            exp_own[:, lanes] = e
            dp_own[:, lanes] = dp
            maxes[0:1, lanes] = top

    def first_root(h, i):
        xi, zi = order[i]
        here = rows(xi, zi)
        key, value = kbuf[h, here, :], vbuf[h, here, :]
        base = at(xi, zi) * SHARD
        for lanes in lane_tiles:
            row = lax.broadcasted_iota(jnp.int32, (SHARD, LT), 0)
            s = jnp.where(row < fork_row[:, lanes] - base, scores(key, h, lanes), NEG)
            before = maxes[i : i + 1, lanes]
            top = jnp.maximum(before, jnp.max(s, axis=0, keepdims=True))
            shrink = jnp.exp2((before - top) * C2)
            e = jnp.exp2(s * C2 - top * C2)
            dp = grads(value, h, lanes)
            total[:, lanes] = total[:, lanes] * shrink + jnp.sum(e, axis=0, keepdims=True)
            corr[:, lanes] = corr[:, lanes] * shrink + jnp.sum(e * dp, axis=0, keepdims=True)
            exp_all[i, :, lanes] = e
            dp_all[i, :, lanes] = dp
            maxes[i + 1 : i + 2, lanes] = top

    def second(h, key, e_ref, dp_ref, i):
        turned = key.T
        count = key.shape[0]
        dk = jnp.zeros((count, HD), F32)
        dv = jnp.zeros((count, HD), F32)
        for lanes in lane_tiles:
            p = e_ref[:, lanes] * maxes[i : i + 1, lanes]
            ds = (p * (dp_ref[:, lanes] - corr[:, lanes])).astype(BF16)
            dk += jnp.dot(ds, qs[h, lanes, :], preferred_element_type=F32)
            dv += jnp.dot(p.astype(BF16), gs[h, lanes, :], preferred_element_type=F32)
            dq_acc[:, lanes] += jnp.dot(turned, ds, preferred_element_type=F32)
        return (dk * SCALE).astype(BF16), dv.astype(BF16)

    def second_root(h, i):
        here = rows(*order[i])
        dk, dv = second(h, kbuf[h, here, :], exp_all.at[i], dp_all.at[i], i + 1)
        pk[h, here, :] = dk
        pv[h, here, :] = dv

    def one_head(h, carry):
        gather3(h)
        first_own(h)
        first_root(h, 0)
        first_root(h, 1)

        @pl.when(h < KVH - 1)
        def _():
            gather1(h + 1)

        @pl.when(h > 0)
        def _():
            reduce2(h - 1)

        first_root(h, 2)
        first_root(h, 3)

        @pl.when(h < KVH - 2)
        def _():
            gather0(h + 2)

        @pl.when(h < KVH - 1)
        def _():
            gather2(h + 1)

        first_root(h, 4)
        first_root(h, 5)

        @pl.when(h > 0)
        def _():
            reduce3(h - 1)

        first_root(h, 6)
        first_root(h, 7)

        inverse = 1.0 / total[...]
        maxes[...] = jnp.exp2((maxes[...] - maxes[N_MEM : N_MEM + 1, :]) * C2) * inverse
        corr[...] = corr[...] * inverse
        dq_acc[...] = jnp.zeros((HD, NQ), F32)
        second_root(h, 0)
        send(h, 23, 17)
        second_root(h, 1)
        send(h, 16)
        second_root(h, 2)
        send(h, 24, 18)
        second_root(h, 3)
        send(h, 25)
        second_root(h, 4)
        send(h, 26)
        second_root(h, 5)
        second_root(h, 6)
        send(h, 19)
        second_root(h, 7)
        dk, dv = second(h, kb_in[:, head_cols(h)], exp_own, dp_own, 0)
        dkb_out[:, head_cols(h)] = dk
        dvb_out[:, head_cols(h)] = dv
        for g in range(GROUP):
            cols = pl.ds(pl.multiple_of((h * GROUP + g) * HD, HD), HD)
            dq_out[:, cols] = (dq_acc[:, g * TOK : (g + 1) * TOK].T * SCALE).astype(BF16)
        reduce1(h)
        return carry

    lax.fori_loop(0, KVH, one_head, 0)
    reduce2(KVH - 1)
    reduce3(KVH - 1)

    def drain(h, carry):
        for slot in range(SLOTS):
            copy(h, slot).wait_send()
        return carry

    lax.fori_loop(0, KVH, drain, 0)


def per_device(*args):
    vmem, anywhere, smem = (
        pl.BlockSpec(memory_space=space) for space in (pltpu.VMEM, pl.ANY, pltpu.SMEM)
    )
    buf = pltpu.VMEM
    return pl.pallas_call(
        kernel,
        out_shape=(
            jax.ShapeDtypeStruct((TOK, KVH * GROUP * HD), BF16),
            jax.ShapeDtypeStruct((TOK, KVH * HD), BF16),
            jax.ShapeDtypeStruct((TOK, KVH * HD), BF16),
            jax.ShapeDtypeStruct((SHARD, KVH * HD), BF16),
            jax.ShapeDtypeStruct((SHARD, KVH * HD), BF16),
        ),
        in_specs=[vmem, vmem, vmem, anywhere, anywhere, vmem, smem, smem],
        out_specs=(vmem,) * 5,
        scratch_shapes=[
            buf((KVH, NQ, HD), BF16),
            buf((KVH, NQ, HD), BF16),
            buf((KVH, ROOT, HD), BF16),
            buf((KVH, ROOT, HD), BF16),
            buf((KVH, ROOT, HD), BF16),
            buf((KVH, ROOT, HD), BF16),
            buf((KVH, 6, SHARD, HD), BF16),
            buf((KVH, SHARD, HD), BF16),
            buf((KVH, 4, SHARD, HD), BF16),
            buf((KVH, 2, HALF, HD), BF16),
            buf((KVH, 2, SHARD, HD), BF16),
            buf((TOK, NQ), F32),
            buf((TOK, NQ), F32),
            buf((N_MEM, SHARD, NQ), F32),
            buf((N_MEM, SHARD, NQ), F32),
            buf((N_MEM + 1, NQ), F32),
            buf((1, NQ), F32),
            buf((1, NQ), F32),
            buf((HD, NQ), F32),
            buf((1, NQ), jnp.int32),
            buf((1, NQ), jnp.int32),
            pltpu.SemaphoreType.DMA((KVH, SLOTS)),
            pltpu.SemaphoreType.DMA((KVH, SLOTS)),
            pltpu.SemaphoreType.DMA((KVH, 2)),
        ],
        compiler_params=pltpu.CompilerParams(
            collective_id=0, has_side_effects=True, vmem_limit_bytes=56 * 2**20
        ),
        cost_estimate=pl.CostEstimate(
            flops=12 * 10**9, bytes_accessed=6 * 10**6, transcendentals=9 * 10**6
        ),
    )(*args)


def solution(mesh):
    spec = P(("grp", "mem"), None)
    return jax.shard_map(
        per_device,
        mesh=mesh,
        in_specs=(spec,) * 8,
        out_specs=(spec,) * 5,
        check_vma=False,
    )
```

```python
import functools
import math

import jax
import jax.numpy as jnp
from jax import lax
from jax.experimental import pallas as pl
from jax.experimental.pallas import tpu as pltpu
from jax.sharding import PartitionSpec as P

KVH = 4
GROUP = 8
HD = 128
TOK = 128
NQ = GROUP * TOK
SHARD = 256
HALF = SHARD // 2
N_MEM = 8
RING = 4
ROOT = SHARD * N_MEM
LT = 256
NEG = -1e30
SCALE = 1.0 / math.sqrt(HD)
C2 = SCALE / math.log(2.0)
SLOTS = 34
QUARTER = SHARD // 4
F32 = jnp.float32
BF16 = jnp.bfloat16
NT = (((1,), (1,)), ((), ()))


def kernel(
    q_in, kb_in, vb_in, kr_in, vr_in, do_in, len_in, fork_in,
    dq_out, dkb_out, dvb_out, dkr_out, dvr_out,
    q_vm, do_vm, dq_vm, small_vm, root_vm,
    qs, gs, kbuf, vbuf, pk, pv, rk, rkx, rvx, rvh, rvf, rvq,
    exp_own, dp_own, exp_all, dp_all, maxes, total, corr, dq_acc, fork_row, start_row,
    ssem, rsem, lsem,
):
    me = lax.axis_index("mem")
    x, z = me // RING, me % RING
    xn = 1 - x
    zp, zm, z2 = (z + 1) % RING, (z + 3) % RING, (z + 2) % RING

    def at(xi, zi):
        return xi * RING + zi

    def rows(xi, zi, first=0, count=SHARD):
        return pl.ds(pl.multiple_of(at(xi, zi) * SHARD + first, QUARTER), count)

    def head_cols(h):
        return pl.ds(pl.multiple_of(h * HD, HD), HD)

    right, left, across = at(x, zp), at(x, zm), at(xn, z)

    def copy(h, slot):
        own_k, own_v = kr_in.at[:, head_cols(h)], vr_in.at[:, head_cols(h)]

        def kv(buf, xi, zi, first=0, count=SHARD):
            return buf.at[h, rows(xi, zi, first, count), :]

        def same(buf, xi, zi, to, first=0, count=SHARD):
            ref = kv(buf, xi, zi, first, count)
            return ref, ref, to

        src, dst, to = {
            0: lambda: (own_k, kv(kbuf, x, z), across),
            1: lambda: (own_k, kv(kbuf, x, z), right),
            2: lambda: (own_k, kv(kbuf, x, z), left),
            3: lambda: same(kbuf, xn, z, right),
            4: lambda: same(kbuf, xn, z, left),
            5: lambda: same(kbuf, x, zm, right),
            6: lambda: same(kbuf, xn, zp, left),
            7: lambda: (own_v, kv(vbuf, x, z), across),
            8: lambda: (own_v, kv(vbuf, x, z), right),
            9: lambda: (own_v, kv(vbuf, x, z), left),
            10: lambda: same(vbuf, x, zm, right, 0, HALF),
            11: lambda: same(vbuf, x, zp, left, HALF, HALF),
            12: lambda: same(vbuf, x, zm, across),
            13: lambda: same(vbuf, x, zp, across),
            14: lambda: same(vbuf, x, z2, across, 0, HALF),
            15: lambda: same(vbuf, xn, zm, right, HALF, QUARTER),
            31: lambda: same(vbuf, xn, zp, left, HALF + QUARTER, QUARTER),
            16: lambda: (kv(pk, x, z2), rk.at[h, 0], right),
            17: lambda: (kv(pk, xn, z2), rk.at[h, 1], left),
            18: lambda: (kv(pk, xn, zp), rk.at[h, 2], right),
            19: lambda: (kv(pk, x, zm), rk.at[h, 3], left),
            20: lambda: (kv(pk, x, zp), rk.at[h, 4], right),
            21: lambda: (kv(pk, xn, zm), rk.at[h, 5], left),
            22: lambda: (kv(pk, xn, z), rkx.at[h], across),
            23: lambda: (kv(pv, xn, z2, 0, HALF), rvx.at[h, 0, pl.ds(0, HALF), :], across),
            32: lambda: (kv(pv, xn, z2, HALF, QUARTER), rvq.at[h, 0], right),
            33: lambda: (kv(pv, xn, z2, HALF + QUARTER, QUARTER), rvq.at[h, 1], left),
            24: lambda: (kv(pv, xn, zp), rvx.at[h, 1], across),
            25: lambda: (kv(pv, xn, zm), rvx.at[h, 2], across),
            26: lambda: (kv(pv, xn, z), rvx.at[h, 3], across),
            27: lambda: (kv(pv, x, z2, 0, HALF), rvh.at[h, 0], right),
            28: lambda: (kv(pv, x, z2, HALF, HALF), rvh.at[h, 1], left),
            29: lambda: (kv(pv, x, zp), rvf.at[h, 0], right),
            30: lambda: (kv(pv, x, zm), rvf.at[h, 1], left),
        }[slot]()
        return pltpu.make_async_remote_copy(
            src_ref=src, dst_ref=dst,
            send_sem=ssem.at[h, slot], recv_sem=rsem.at[h, slot],
            device_id={"mem": to}, device_id_type=pl.DeviceIdType.MESH,
        )

    def send(h, *slots):
        for slot in slots:
            copy(h, slot).start()

    def arrive(h, *slots):
        for slot in slots:
            copy(h, slot).wait_recv()

    def wide_cols(h):
        return pl.ds(pl.multiple_of(h * NQ, NQ), NQ)

    def local(h, which):
        thin, wide, own = head_cols(h), wide_cols(h), rows(x, z)
        src, dst = (
            (kr_in.at[:, thin], kbuf.at[h, own, :]),
            (vr_in.at[:, thin], vbuf.at[h, own, :]),
            (q_in.at[:, wide], q_vm.at[:, wide]),
            (do_in.at[:, wide], do_vm.at[:, wide]),
            (dq_vm.at[:, wide], dq_out.at[:, wide]),
            (small_vm.at[0, h], dkb_out.at[:, thin]),
            (small_vm.at[1, h], dvb_out.at[:, thin]),
            (root_vm.at[0, h], dkr_out.at[:, thin]),
            (root_vm.at[1, h], dvr_out.at[:, thin]),
        )[which]
        return pltpu.make_async_copy(src, dst, lsem.at[h, which])

    def gather0(h):
        send(h, 0, 8, 9, 7, 1, 2)

    def gather1(h):
        arrive(h, 0)
        send(h, 3, 4)
        arrive(h, 8)
        send(h, 12, 10)
        arrive(h, 9)
        send(h, 13, 11)
        arrive(h, 1)
        send(h, 5)

    def gather2(h):
        arrive(h, 4)
        send(h, 6)
        arrive(h, 10)
        send(h, 14)
        arrive(h, 12)
        send(h, 15)
        arrive(h, 13)
        send(h, 31)

    def f32(ref):
        return ref.astype(F32)

    def reduce0(h):
        for side, zi, first in ((0, zp, HALF), (1, zm, HALF + QUARTER)):
            arrive(h, 32 + side)
            here = rows(xn, zi, first, QUARTER)
            pv[h, here, :] = (f32(pv[h, here, :]) + f32(rvq[h, side])).astype(BF16)
            send(h, 24 + side)

    def reduce1(h):
        arrive(h, 23)
        here = rows(x, z2, 0, HALF)
        pv[h, here, :] = (f32(pv[h, here, :]) + f32(rvx[h, 0, :HALF])).astype(BF16)
        send(h, 27)
        arrive(h, 16)
        here = rows(x, zp)
        pk[h, here, :] = (f32(pk[h, here, :]) + f32(rk[h, 0])).astype(BF16)
        send(h, 20)
        arrive(h, 17)
        here = rows(xn, zm)
        pk[h, here, :] = (f32(pk[h, here, :]) + f32(rk[h, 1])).astype(BF16)
        send(h, 21)

    def reduce2(h):
        arrive(h, 24, 25, 27, 28)
        here, rest = rows(x, zp, 0, HALF), rows(x, zp, HALF, HALF)
        pv[h, here, :] = (f32(pv[h, here, :]) + f32(rvx[h, 1, :HALF]) + f32(rvh[h, 0])).astype(BF16)
        pv[h, rest, :] = (f32(pv[h, rest, :]) + f32(rvx[h, 1, HALF:])).astype(BF16)
        send(h, 29)
        here, rest = rows(x, zm, HALF, HALF), rows(x, zm, 0, HALF)
        pv[h, here, :] = (f32(pv[h, here, :]) + f32(rvx[h, 2, HALF:]) + f32(rvh[h, 1])).astype(BF16)
        pv[h, rest, :] = (f32(pv[h, rest, :]) + f32(rvx[h, 2, :HALF])).astype(BF16)
        send(h, 30)
        arrive(h, 18, 21)
        here = rows(xn, z)
        pk[h, here, :] = (f32(pk[h, here, :]) + f32(rk[h, 2]) + f32(rk[h, 5])).astype(BF16)
        send(h, 22)

    def reduce3(h):
        own = rows(x, z)
        arrive(h, 26, 29, 30)
        root_vm[1, h] = (
            f32(pv[h, own, :]) + f32(rvx[h, 3]) + f32(rvf[h, 0]) + f32(rvf[h, 1])
        ).astype(BF16)
        arrive(h, 19, 20, 22)
        local(h, 8).start()
        root_vm[0, h] = (
            f32(pk[h, own, :]) + f32(rk[h, 3]) + f32(rk[h, 4]) + f32(rkx[h])
        ).astype(BF16)
        local(h, 7).start()

    barrier = pltpu.get_barrier_semaphore()
    for peer in (right, left, across):
        pl.semaphore_signal(
            barrier, inc=1, device_id={"mem": peer}, device_id_type=pl.DeviceIdType.MESH
        )
    for h in range(KVH):
        for which in range(4):
            local(h, which).start()
    pl.semaphore_wait(barrier, 3)
    gather0(0)
    gather0(1)

    lens = [len_in[0, b] for b in range(4)]
    ends = [lens[0], lens[0] + lens[1], lens[0] + lens[1] + lens[2]]
    place = lax.broadcasted_iota(jnp.int32, (1, NQ), 1) % TOK
    fork = jnp.full((1, NQ), fork_in[0, 0], jnp.int32)
    start = jnp.zeros((1, NQ), jnp.int32)
    for b, end in enumerate(ends):
        fork = jnp.where(place >= end, fork_in[0, b + 1], fork)
        start = jnp.where(place >= end, end, start)
    fork_row[...] = fork
    start_row[...] = start

    def lay_out(h):
        local(h, 2).wait()
        local(h, 3).wait()
        for g in range(GROUP):
            cols = pl.ds(pl.multiple_of((h * GROUP + g) * HD, HD), HD)
            qs[h, g * TOK : (g + 1) * TOK, :] = q_vm[:, cols]
            gs[h, g * TOK : (g + 1) * TOK, :] = do_vm[:, cols]

    order = [
        (x, z), (xn, z), (x, zp), (x, zm), (xn, zp), (xn, zm), (x, z2), (xn, z2),
    ]

    def scores(key, h, lanes):
        return lax.dot_general(key, qs[h, lanes, :], NT, preferred_element_type=F32)

    def grads(value, h, lanes):
        return lax.dot_general(value, gs[h, lanes, :], NT, preferred_element_type=F32)

    lane_tiles = [slice(t, t + LT) for t in range(0, NQ, LT)]

    def first_own(h, par):
        key, value = kb_in[:, head_cols(h)], vb_in[:, head_cols(h)]
        for lanes in lane_tiles:
            row = lax.broadcasted_iota(jnp.int32, (TOK, LT), 0)
            lane = lax.broadcasted_iota(jnp.int32, (TOK, LT), 1) % TOK
            seen = (row <= lane) & (row >= start_row[:, lanes])
            s = jnp.where(seen, scores(key, h, lanes), NEG)
            top = jnp.max(s, axis=0, keepdims=True)
            e = jnp.exp2(s * C2 - top * C2)
            dp = grads(value, h, lanes)
            total[par, :, lanes] = jnp.sum(e, axis=0, keepdims=True)
            corr[par, :, lanes] = jnp.sum(e * dp, axis=0, keepdims=True)
            exp_own[par, :, lanes] = e
            dp_own[par, :, lanes] = dp
            maxes[par, 0:1, lanes] = top

    def first_root(h, par, i, shard):
        here = pl.ds(pl.multiple_of(shard * SHARD, SHARD), SHARD)
        key, value = kbuf[h, here, :], vbuf[h, here, :]
        base = shard * SHARD
        for lanes in lane_tiles:
            row = lax.broadcasted_iota(jnp.int32, (SHARD, LT), 0)
            s = jnp.where(row < fork_row[:, lanes] - base, scores(key, h, lanes), NEG)
            before = maxes[par, pl.ds(i, 1), lanes]
            top = jnp.maximum(before, jnp.max(s, axis=0, keepdims=True))
            shrink = jnp.exp2((before - top) * C2)
            e = jnp.exp2(s * C2 - top * C2)
            dp = grads(value, h, lanes)
            total[par, :, lanes] = total[par, :, lanes] * shrink + jnp.sum(e, axis=0, keepdims=True)
            corr[par, :, lanes] = corr[par, :, lanes] * shrink + jnp.sum(e * dp, axis=0, keepdims=True)
            exp_all[par, i, :, lanes] = e
            dp_all[par, i, :, lanes] = dp
            maxes[par, pl.ds(i + 1, 1), lanes] = top

    def second(h, par, key, e_ref, dp_ref, i):
        turned = key.T
        count = key.shape[0]
        dk = jnp.zeros((count, HD), F32)
        dv = jnp.zeros((count, HD), F32)
        for lanes in lane_tiles:
            p = e_ref[:, lanes] * maxes[par, pl.ds(i, 1), lanes]
            ds = (p * (dp_ref[:, lanes] - corr[par, :, lanes])).astype(BF16)
            dk += jnp.dot(ds, qs[h, lanes, :], preferred_element_type=F32)
            dv += jnp.dot(p.astype(BF16), gs[h, lanes, :], preferred_element_type=F32)
            dq_acc[:, lanes] += jnp.dot(turned, ds, preferred_element_type=F32)
        return (dk * SCALE).astype(BF16), dv.astype(BF16)

    def second_root(h, par, i, shard):
        here = pl.ds(pl.multiple_of(shard * SHARD, SHARD), SHARD)
        dk, dv = second(h, par, kbuf[h, here, :], exp_all.at[par, i], dp_all.at[par, i], i + 1)
        pk[h, here, :] = dk
        pv[h, here, :] = dv

    def when(condition, step, *args):
        @pl.when(condition)
        def _():
            step(*args)

    shards = [at(xi, zi) for xi, zi in order]

    def step(s, carry):
        now, after = s - 1, s
        odd = s % 2
        even = 1 - odd

        @pl.when(s < KVH)
        def _():
            lay_out(after)
            first_own(after, odd)

        @pl.when(s == 0)
        def _():
            for h in range(KVH):
                local(h, 0).wait()
                local(h, 1).wait()
            gather1(0)
            gather1(1)

        when(s == 1, gather0, 3)

        def first_group(far, carry):
            h = s - far
            par = (odd + far) % 2
            when(far == 0, arrive, h, 7)
            when(far == 1, arrive, h, 3)
            for c in range(4):
                if c == 2:

                    @pl.when((far == 0) & (s == 0))
                    def _():
                        gather2(0)
                        gather0(2)

                    when(far == 0, arrive, h, 2)
                    when(far == 1, arrive, h, 5, 11, 6, 14, 15, 31)
                first_root(h, par, far * 4 + c, jnp.where(far == 0, shards[c], shards[4 + c]))
            when((far == 0) & (s == 2), gather2, 2)
            return carry

        lax.fori_loop(jnp.where(s == KVH, 1, 0), jnp.where(s == 0, 1, 2), first_group, 0)

        def second_half():
            h = now
            inverse = 1.0 / total[even]
            maxes[even] = jnp.exp2((maxes[even] - maxes[even, N_MEM : N_MEM + 1, :]) * C2) * inverse
            corr[even] = corr[even] * inverse
            dq_acc[...] = jnp.zeros((HD, NQ), F32)

            def second_group(near, carry):
                for c, (i, j) in enumerate(((7, 2), (6, 3), (4, 1), (5, 0))):
                    second_root(
                        h, even, jnp.where(near == 0, i, j),
                        jnp.where(near == 0, shards[i], shards[j]),
                    )
                    if c == 1:
                        when(near == 0, send, h, 23, 17, 16, 32, 33, 28)
                        when(near == 1, send, h, 19)

                        @pl.when((near == 0) & (s == 2 - 1))
                        def _():
                            gather2(1)
                            gather1(2)

                        when((near == 0) & (s == 3), gather2, 3)
                when(near == 0, send, h, 18)
                when(near == 1, send, h, 26)
                when((near == 0) & (s == 2), gather1, 3)
                return carry

            lax.fori_loop(0, 2, second_group, 0)
            dk, dv = second(h, even, kb_in[:, head_cols(h)], exp_own.at[even], dp_own.at[even], 0)
            small_vm[0, h] = dk
            small_vm[1, h] = dv
            local(h, 5).start()
            local(h, 6).start()
            for g in range(GROUP):
                cols = pl.ds(pl.multiple_of((h * GROUP + g) * HD, HD), HD)
                dq_vm[:, cols] = (dq_acc[:, g * TOK : (g + 1) * TOK].T * SCALE).astype(BF16)
            local(h, 4).start()
            reduce0(h)
            reduce1(h)

        when(s > 0, second_half)
        when(s > 1, reduce2, s - 2)
        when(s > 2, reduce3, s - 3)
        return carry

    lax.fori_loop(0, KVH + 1, step, 0)
    reduce2(KVH - 1)
    reduce3(KVH - 2)
    reduce3(KVH - 1)

    def drain(h, carry):
        for slot in range(SLOTS):
            copy(h, slot).wait_send()
        for which in range(4, 9):
            local(h, which).wait()
        return carry

    lax.fori_loop(0, KVH, drain, 0)


def hand_over(dq, dkb, dvb, dkr, dvr, dq_out, dkb_out, dvb_out, dkr_out, dvr_out, *rest):
    *held, came, gone = rest
    srcs, dsts = (dq, dkb, dvb, dkr, dvr), (dq_out, dkb_out, dvb_out, dkr_out, dvr_out)
    ins = [pltpu.make_async_copy(a, b, came.at[i]) for i, (a, b) in enumerate(zip(srcs, held))]
    outs = [pltpu.make_async_copy(a, b, gone.at[i]) for i, (a, b) in enumerate(zip(held, dsts))]
    for one in ins:
        one.start()
    for one, other in zip(ins, outs):
        one.wait()
        other.start()
    for other in outs:
        other.wait()


def per_device(*args):
    vmem, anywhere, smem = (
        pl.BlockSpec(memory_space=space) for space in (pltpu.VMEM, pl.ANY, pltpu.SMEM)
    )
    buf = pltpu.VMEM
    outs = pl.pallas_call(
        kernel,
        out_shape=(
            jax.ShapeDtypeStruct((TOK, KVH * GROUP * HD), BF16),
            jax.ShapeDtypeStruct((TOK, KVH * HD), BF16),
            jax.ShapeDtypeStruct((TOK, KVH * HD), BF16),
            jax.ShapeDtypeStruct((SHARD, KVH * HD), BF16),
            jax.ShapeDtypeStruct((SHARD, KVH * HD), BF16),
        ),
        in_specs=[anywhere, vmem, vmem, anywhere, anywhere, anywhere, smem, smem],
        out_specs=(anywhere,) * 5,
        scratch_shapes=[
            buf((TOK, KVH * NQ), BF16),
            buf((TOK, KVH * NQ), BF16),
            buf((TOK, KVH * NQ), BF16),
            buf((2, KVH, TOK, HD), BF16),
            buf((2, KVH, SHARD, HD), BF16),
            buf((KVH, NQ, HD), BF16),
            buf((KVH, NQ, HD), BF16),
            buf((KVH, ROOT, HD), BF16),
            buf((KVH, ROOT, HD), BF16),
            buf((KVH, ROOT, HD), BF16),
            buf((KVH, ROOT, HD), BF16),
            buf((KVH, 6, SHARD, HD), BF16),
            buf((KVH, SHARD, HD), BF16),
            buf((KVH, 4, SHARD, HD), BF16),
            buf((KVH, 2, HALF, HD), BF16),
            buf((KVH, 2, SHARD, HD), BF16),
            buf((KVH, 2, QUARTER, HD), BF16),
            buf((2, TOK, NQ), F32),
            buf((2, TOK, NQ), F32),
            buf((2, N_MEM, SHARD, NQ), F32),
            buf((2, N_MEM, SHARD, NQ), F32),
            buf((2, N_MEM + 1, NQ), F32),
            buf((2, 1, NQ), F32),
            buf((2, 1, NQ), F32),
            buf((HD, NQ), F32),
            buf((1, NQ), jnp.int32),
            buf((1, NQ), jnp.int32),
            pltpu.SemaphoreType.DMA((KVH, SLOTS)),
            pltpu.SemaphoreType.DMA((KVH, SLOTS)),
            pltpu.SemaphoreType.DMA((KVH, 9)),
        ],
        compiler_params=pltpu.CompilerParams(
            collective_id=0, has_side_effects=True, vmem_limit_bytes=60 * 2**20
        ),
        cost_estimate=pl.CostEstimate(
            flops=12 * 10**9, bytes_accessed=6 * 10**6, transcendentals=9 * 10**6
        ),
    )(*args)
    return pl.pallas_call(
        hand_over,
        out_shape=tuple(jax.ShapeDtypeStruct(out.shape, out.dtype) for out in outs),
        in_specs=[anywhere] * 5,
        out_specs=(anywhere,) * 5,
        scratch_shapes=[pltpu.VMEM(out.shape, out.dtype) for out in outs]
        + [pltpu.SemaphoreType.DMA((5,))] * 2,
    )(*outs)


def solution(mesh):
    spec = P(("grp", "mem"), None)
    return jax.shard_map(
        per_device,
        mesh=mesh,
        in_specs=(spec,) * 8,
        out_specs=(spec,) * 5,
        check_vma=False,
    )
```

```python
import functools
import math

import jax
import jax.numpy as jnp
from jax import lax
from jax.experimental import pallas as pl
from jax.experimental.pallas import tpu as pltpu
from jax.sharding import PartitionSpec as P

KVH = 4
GROUP = 8
HD = 128
TOK = 128
NQ = GROUP * TOK
SHARD = 256
HALF = SHARD // 2
N_MEM = 8
RING = 4
ROOT = SHARD * N_MEM
LT = 256
NEG = -1e30
SCALE = 1.0 / math.sqrt(HD)
C2 = SCALE / math.log(2.0)
SLOTS = 34
START, OWN, NEAR_A, NEAR_B, FAR_A, FAR_B, BACK_A, BACK_B, BACK_C, BACK_D, DONE = range(11)
PLAN = {
    (START, 0): [(1, 0), (0, 0), (3, 0), (1, 1), (3, 1), (2, 1), (2, 0), (5, 0), (4, 0)],
    (OWN, 0): [(7, 0), (6, 0), (0, 1), (1, 2)],
    (NEAR_A, 0): [(6, 1)],
    (NEAR_B, 0): [(8, 0), (9, 0), (0, 2), (5, 1), (10, 0), (0, 3), (11, 0), (2, 2), (4, 1)],
    (OWN, 1): [(1, 3)],
    (NEAR_A, 1): [(7, 1), (11, 1)],
    (NEAR_B, 1): [(6, 2), (3, 2)],
    (FAR_B, 0): [(9, 1), (4, 2), (8, 1)],
    (BACK_A, 0): [(10, 1), (5, 2)],
    (OWN, 2): [(2, 3), (3, 3), (6, 3)],
    (NEAR_A, 2): [(4, 3), (7, 2), (8, 2)],
    (FAR_A, 1): [(5, 3), (11, 2), (10, 2)],
    (BACK_A, 1): [(9, 2)],
    (BACK_D, 1): [(11, 3), (7, 3)],
    (OWN, 3): [(15, 0)],
    (NEAR_A, 3): [(12, 0), (13, 0), (16, 0), (9, 3)],
    (FAR_B, 2): [(14, 0), (8, 3), (10, 3), (12, 1)],
    (BACK_B, 2): [(13, 1)],
    (BACK_C, 2): [(16, 1)],
    (BACK_D, 2): [(17, 0), (14, 1)],
    (FAR_A, 3): [(15, 2), (19, 0)],
    (FAR_B, 3): [(16, 2), (12, 2)],
    (BACK_A, 3): [(13, 2), (14, 2), (18, 1), (15, 1)],
    (BACK_B, 3): [(19, 1), (14, 3), (17, 1), (18, 0), (12, 3), (13, 3), (21, 0), (16, 3)],
    (BACK_C, 3): [(17, 2)],
    (BACK_D, 3): [(15, 3), (18, 2), (19, 2), (17, 3), (20, 0), (21, 1), (19, 3), (18, 3)],
    (DONE, 3): [(20, 2), (21, 2), (20, 1), (21, 3), (20, 3)],
}
QUARTER = SHARD // 4
F32 = jnp.float32
BF16 = jnp.bfloat16
NT = (((1,), (1,)), ((), ()))


def kernel(
    q_in, kb_in, vb_in, kr_in, vr_in, do_in, len_in, fork_in,
    dq_out, dkb_out, dvb_out, dkr_out, dvr_out,
    q_vm, do_vm, dq_vm, small_vm, root_vm,
    qs, gs, kbuf, vbuf, pk, pv, rk, rkx, rvx, rvh, rvf, rvq,
    exp_own, dp_own, exp_all, dp_all, maxes, total, corr, dq_acc, fork_row, start_row,
    ssem, rsem, lsem,
):
    me = lax.axis_index("mem")
    x, z = me // RING, me % RING
    xn = 1 - x
    zp, zm, z2 = (z + 1) % RING, (z + 3) % RING, (z + 2) % RING

    def at(xi, zi):
        return xi * RING + zi

    def rows(xi, zi, first=0, count=SHARD):
        return pl.ds(pl.multiple_of(at(xi, zi) * SHARD + first, QUARTER), count)

    def head_cols(h):
        return pl.ds(pl.multiple_of(h * HD, HD), HD)

    right, left, across = at(x, zp), at(x, zm), at(xn, z)

    def copy(h, slot):
        own_k, own_v = kr_in.at[:, head_cols(h)], vr_in.at[:, head_cols(h)]

        def kv(buf, xi, zi, first=0, count=SHARD):
            return buf.at[h, rows(xi, zi, first, count), :]

        def same(buf, xi, zi, to, first=0, count=SHARD):
            ref = kv(buf, xi, zi, first, count)
            return ref, ref, to

        src, dst, to = {
            0: lambda: (own_k, kv(kbuf, x, z), across),
            1: lambda: (own_k, kv(kbuf, x, z), right),
            2: lambda: (own_k, kv(kbuf, x, z), left),
            3: lambda: same(kbuf, xn, z, right),
            4: lambda: same(kbuf, xn, z, left),
            5: lambda: same(kbuf, x, zm, right),
            6: lambda: same(kbuf, xn, zp, left),
            7: lambda: (own_v, kv(vbuf, x, z), across),
            8: lambda: (own_v, kv(vbuf, x, z), right),
            9: lambda: (own_v, kv(vbuf, x, z), left),
            10: lambda: same(vbuf, x, zm, right, 0, HALF),
            11: lambda: same(vbuf, x, zp, left, HALF, HALF),
            12: lambda: same(vbuf, x, zm, across),
            13: lambda: same(vbuf, x, zp, across),
            14: lambda: same(vbuf, x, z2, across, 0, HALF),
            15: lambda: same(vbuf, xn, zm, right, HALF, QUARTER),
            31: lambda: same(vbuf, xn, zp, left, HALF + QUARTER, QUARTER),
            16: lambda: (kv(pk, x, z2), rk.at[h, 0], right),
            17: lambda: (kv(pk, xn, z2), rk.at[h, 1], left),
            18: lambda: (kv(pk, xn, zp), rk.at[h, 2], right),
            19: lambda: (kv(pk, x, zm), rk.at[h, 3], left),
            20: lambda: (kv(pk, x, zp), rk.at[h, 4], right),
            21: lambda: (kv(pk, xn, zm), rk.at[h, 5], left),
            22: lambda: (kv(pk, xn, z), rkx.at[h], across),
            23: lambda: (kv(pv, xn, z2, 0, HALF), rvx.at[h, 0, pl.ds(0, HALF), :], across),
            32: lambda: (kv(pv, xn, z2, HALF, QUARTER), rvq.at[h, 0], right),
            33: lambda: (kv(pv, xn, z2, HALF + QUARTER, QUARTER), rvq.at[h, 1], left),
            24: lambda: (kv(pv, xn, zp), rvx.at[h, 1], across),
            25: lambda: (kv(pv, xn, zm), rvx.at[h, 2], across),
            26: lambda: (kv(pv, xn, z), rvx.at[h, 3], across),
            27: lambda: (kv(pv, x, z2, 0, HALF), rvh.at[h, 0], right),
            28: lambda: (kv(pv, x, z2, HALF, HALF), rvh.at[h, 1], left),
            29: lambda: (kv(pv, x, zp), rvf.at[h, 0], right),
            30: lambda: (kv(pv, x, zm), rvf.at[h, 1], left),
        }[slot]()
        return pltpu.make_async_remote_copy(
            src_ref=src, dst_ref=dst,
            send_sem=ssem.at[h, slot], recv_sem=rsem.at[h, slot],
            device_id={"mem": to}, device_id_type=pl.DeviceIdType.MESH,
        )

    def send(h, *slots):
        for slot in slots:
            copy(h, slot).start()

    def arrive(h, *slots):
        for slot in slots:
            copy(h, slot).wait_recv()

    def wide_cols(h):
        return pl.ds(pl.multiple_of(h * NQ, NQ), NQ)

    def local(h, which):
        thin, wide, own = head_cols(h), wide_cols(h), rows(x, z)
        src, dst = (
            (kr_in.at[:, thin], kbuf.at[h, own, :]),
            (vr_in.at[:, thin], vbuf.at[h, own, :]),
            (q_in.at[:, wide], q_vm.at[:, wide]),
            (do_in.at[:, wide], do_vm.at[:, wide]),
            (dq_vm.at[:, wide], dq_out.at[:, wide]),
            (small_vm.at[0, h], dkb_out.at[:, thin]),
            (small_vm.at[1, h], dvb_out.at[:, thin]),
            (root_vm.at[0, h], dkr_out.at[:, thin]),
            (root_vm.at[1, h], dvr_out.at[:, thin]),
        )[which]
        return pltpu.make_async_copy(src, dst, lsem.at[h, which])

    def f32(ref):
        return ref.astype(F32)

    def plus(buf, h, here, *terms):
        total_here = f32(buf[h, here, :])
        for term in terms:
            total_here = total_here + f32(term)
        buf[h, here, :] = total_here.astype(BF16)

    def pass_on(h, waits, sends):
        arrive(h, *waits)
        send(h, *sends)

    def value_side(h, side):
        arrive(h, 32 + side)
        zi, first = ((zp, HALF), (zm, HALF + QUARTER))[side]
        plus(pv, h, rows(xn, zi, first, QUARTER), rvq[h, side])
        send(h, 24 + side)

    def value_half(h):
        arrive(h, 23)
        plus(pv, h, rows(x, z2, 0, HALF), rvx[h, 0, :HALF])
        send(h, 27)

    def key_side(h, side):
        arrive(h, 16 + side)
        plus(pk, h, (rows(x, zp), rows(xn, zm))[side], rk[h, side])
        send(h, 20 + side)

    def value_block(h, side):
        arrive(h, 24 + side, 27 + side)
        zi = (zp, zm)[side]
        first, other = ((0, HALF), (HALF, 0))[side]
        plus(pv, h, rows(x, zi, first, HALF), rvx[h, 1 + side, first : first + HALF], rvh[h, side])
        plus(pv, h, rows(x, zi, other, HALF), rvx[h, 1 + side, other : other + HALF])
        send(h, 29 + side)

    def key_across(h):
        arrive(h, 18, 21)
        plus(pk, h, rows(xn, z), rk[h, 2], rk[h, 5])
        send(h, 22)

    def value_out(h):
        arrive(h, 26, 29, 30)
        root_vm[1, h] = (
            f32(pv[h, rows(x, z), :]) + f32(rvx[h, 3]) + f32(rvf[h, 0]) + f32(rvf[h, 1])
        ).astype(BF16)
        local(h, 8).start()

    def key_out(h):
        arrive(h, 19, 20, 22)
        root_vm[0, h] = (
            f32(pk[h, rows(x, z), :]) + f32(rk[h, 3]) + f32(rk[h, 4]) + f32(rkx[h])
        ).astype(BF16)
        local(h, 7).start()

    steps = [
        lambda h: send(h, 0),
        lambda h: send(h, 8, 9),
        lambda h: send(h, 7),
        lambda h: send(h, 1, 2),
        lambda h: pass_on(h, (0,), (3, 4)),
        lambda h: pass_on(h, (8,), (12, 10)),
        lambda h: pass_on(h, (9,), (13, 11)),
        lambda h: pass_on(h, (1,), (5,)),
        lambda h: pass_on(h, (4,), (6,)),
        lambda h: pass_on(h, (10,), (14,)),
        lambda h: pass_on(h, (12,), (15,)),
        lambda h: pass_on(h, (13,), (31,)),
        lambda h: value_side(h, 0),
        lambda h: value_side(h, 1),
        value_half,
        lambda h: key_side(h, 0),
        lambda h: key_side(h, 1),
        lambda h: value_block(h, 0),
        lambda h: value_block(h, 1),
        key_across,
        value_out,
        key_out,
    ]

    def run(piece, head):
        for number, h in PLAN.get((piece, head), ()):
            steps[number](h)

    def run_when(piece, head, guard=None):
        for h in range(KVH):
            if (piece, h) in PLAN:

                @pl.when(head == h if guard is None else (head == h) & guard)
                def _():
                    run(piece, h)

    barrier = pltpu.get_barrier_semaphore()
    for peer in (right, left, across):
        pl.semaphore_signal(
            barrier, inc=1, device_id={"mem": peer}, device_id_type=pl.DeviceIdType.MESH
        )
    for h in range(KVH):
        for which in range(4):
            local(h, which).start()
    lens = [len_in[0, b] for b in range(4)]
    ends = [lens[0], lens[0] + lens[1], lens[0] + lens[1] + lens[2]]
    place = lax.broadcasted_iota(jnp.int32, (1, NQ), 1) % TOK
    fork = jnp.full((1, NQ), fork_in[0, 0], jnp.int32)
    start = jnp.zeros((1, NQ), jnp.int32)
    for b, end in enumerate(ends):
        fork = jnp.where(place >= end, fork_in[0, b + 1], fork)
        start = jnp.where(place >= end, end, start)
    fork_row[...] = fork
    start_row[...] = start

    def lay_out(h):
        local(h, 2).wait()
        local(h, 3).wait()
        for g in range(GROUP):
            cols = pl.ds(pl.multiple_of((h * GROUP + g) * HD, HD), HD)
            qs[h, g * TOK : (g + 1) * TOK, :] = q_vm[:, cols]
            gs[h, g * TOK : (g + 1) * TOK, :] = do_vm[:, cols]

    lay_out(0)
    for h in range(KVH):
        local(h, 0).wait()
        local(h, 1).wait()
    pl.semaphore_wait(barrier, 3)
    run(START, 0)

    order = [
        (x, z), (xn, z), (x, zp), (x, zm), (xn, zp), (xn, zm), (x, z2), (xn, z2),
    ]

    def scores(key, h, lanes):
        return lax.dot_general(key, qs[h, lanes, :], NT, preferred_element_type=F32)

    def grads(value, h, lanes):
        return lax.dot_general(value, gs[h, lanes, :], NT, preferred_element_type=F32)

    lane_tiles = [slice(t, t + LT) for t in range(0, NQ, LT)]

    def first_own(h, par):
        key, value = kb_in[:, head_cols(h)], vb_in[:, head_cols(h)]
        for lanes in lane_tiles:
            row = lax.broadcasted_iota(jnp.int32, (TOK, LT), 0)
            lane = lax.broadcasted_iota(jnp.int32, (TOK, LT), 1) % TOK
            seen = (row <= lane) & (row >= start_row[:, lanes])
            s = jnp.where(seen, scores(key, h, lanes), NEG)
            top = jnp.max(s, axis=0, keepdims=True)
            e = jnp.exp2(s * C2 - top * C2)
            dp = grads(value, h, lanes)
            total[par, :, lanes] = jnp.sum(e, axis=0, keepdims=True)
            corr[par, :, lanes] = jnp.sum(e * dp, axis=0, keepdims=True)
            exp_own[par, :, lanes] = e
            dp_own[par, :, lanes] = dp
            maxes[par, 0:1, lanes] = top

    def first_root(h, par, i, shard):
        here = pl.ds(pl.multiple_of(shard * SHARD, SHARD), SHARD)
        key, value = kbuf[h, here, :], vbuf[h, here, :]
        base = shard * SHARD
        for lanes in lane_tiles:
            row = lax.broadcasted_iota(jnp.int32, (SHARD, LT), 0)
            s = jnp.where(row < fork_row[:, lanes] - base, scores(key, h, lanes), NEG)
            before = maxes[par, pl.ds(i, 1), lanes]
            top = jnp.maximum(before, jnp.max(s, axis=0, keepdims=True))
            shrink = jnp.exp2((before - top) * C2)
            e = jnp.exp2(s * C2 - top * C2)
            dp = grads(value, h, lanes)
            total[par, :, lanes] = total[par, :, lanes] * shrink + jnp.sum(e, axis=0, keepdims=True)
            corr[par, :, lanes] = corr[par, :, lanes] * shrink + jnp.sum(e * dp, axis=0, keepdims=True)
            exp_all[par, i, :, lanes] = e
            dp_all[par, i, :, lanes] = dp
            maxes[par, pl.ds(i + 1, 1), lanes] = top

    def second(h, par, key, e_ref, dp_ref, i):
        turned = key.T
        count = key.shape[0]
        dk = jnp.zeros((count, HD), F32)
        dv = jnp.zeros((count, HD), F32)
        for lanes in lane_tiles:
            p = e_ref[:, lanes] * maxes[par, pl.ds(i, 1), lanes]
            ds = (p * (dp_ref[:, lanes] - corr[par, :, lanes])).astype(BF16)
            dk += jnp.dot(ds, qs[h, lanes, :], preferred_element_type=F32)
            dv += jnp.dot(p.astype(BF16), gs[h, lanes, :], preferred_element_type=F32)
            dq_acc[:, lanes] += jnp.dot(turned, ds, preferred_element_type=F32)
        return (dk * SCALE).astype(BF16), dv.astype(BF16)

    def second_root(h, par, i, shard):
        here = pl.ds(pl.multiple_of(shard * SHARD, SHARD), SHARD)
        dk, dv = second(h, par, kbuf[h, here, :], exp_all.at[par, i], dp_all.at[par, i], i + 1)
        pk[h, here, :] = dk
        pv[h, here, :] = dv

    def when(condition, step, *args):
        @pl.when(condition)
        def _():
            step(*args)

    shards = [at(xi, zi) for xi, zi in order]

    def step(s, carry):
        now, after = s - 1, s
        odd = s % 2
        even = 1 - odd

        @pl.when(s < KVH)
        def _():
            first_own(after, odd)

        @pl.when(s < KVH - 1)
        def _():
            lay_out(s + 1)

        run_when(OWN, s)

        def first_group(far, carry):
            h = s - far
            par = (odd + far) % 2
            when(far == 0, arrive, h, 7)
            when(far == 1, arrive, h, 3)
            for c in range(4):
                if c == 2:

                    run_when(NEAR_A, h, far == 0)
                    run_when(FAR_A, h, far == 1)
                    when(far == 0, arrive, h, 2)
                    when(far == 1, arrive, h, 5, 11, 6, 14, 15, 31)
                first_root(h, par, far * 4 + c, jnp.where(far == 0, shards[c], shards[4 + c]))
            run_when(NEAR_B, h, far == 0)
            run_when(FAR_B, h, far == 1)
            return carry

        lax.fori_loop(jnp.where(s == KVH, 1, 0), jnp.where(s == 0, 1, 2), first_group, 0)

        def second_half():
            h = now
            inverse = 1.0 / total[even]
            maxes[even] = jnp.exp2((maxes[even] - maxes[even, N_MEM : N_MEM + 1, :]) * C2) * inverse
            corr[even] = corr[even] * inverse
            dq_acc[...] = jnp.zeros((HD, NQ), F32)

            def second_group(near, carry):
                for c, (i, j) in enumerate(((7, 2), (6, 3), (4, 1), (5, 0))):
                    second_root(
                        h, even, jnp.where(near == 0, i, j),
                        jnp.where(near == 0, shards[i], shards[j]),
                    )
                    if c == 1:
                        when(near == 0, send, h, 23, 17, 16, 32, 33, 28)
                        when(near == 1, send, h, 19)

                        run_when(BACK_A, h, near == 0)
                        run_when(BACK_C, h, near == 1)
                when(near == 0, send, h, 18)
                when(near == 1, send, h, 26)
                run_when(BACK_B, h, near == 0)
                run_when(BACK_D, h, near == 1)
                return carry

            lax.fori_loop(0, 2, second_group, 0)
            dk, dv = second(h, even, kb_in[:, head_cols(h)], exp_own.at[even], dp_own.at[even], 0)
            small_vm[0, h] = dk
            small_vm[1, h] = dv
            local(h, 5).start()
            local(h, 6).start()
            for g in range(GROUP):
                cols = pl.ds(pl.multiple_of((h * GROUP + g) * HD, HD), HD)
                dq_vm[:, cols] = (dq_acc[:, g * TOK : (g + 1) * TOK].T * SCALE).astype(BF16)
            local(h, 4).start()
            run_when(DONE, h)

        when(s > 0, second_half)
        return carry

    lax.fori_loop(0, KVH + 1, step, 0)

    def drain(h, carry):
        for slot in range(SLOTS):
            copy(h, slot).wait_send()
        for which in range(4, 9):
            local(h, which).wait()
        return carry

    lax.fori_loop(0, KVH, drain, 0)


def hand_over(dq, dkb, dvb, dkr, dvr, dq_out, dkb_out, dvb_out, dkr_out, dvr_out, gone):
    srcs, dsts = (dq, dkb, dvb, dkr, dvr), (dq_out, dkb_out, dvb_out, dkr_out, dvr_out)
    outs = [pltpu.make_async_copy(a, b, gone.at[i]) for i, (a, b) in enumerate(zip(srcs, dsts))]
    for one in outs:
        one.start()
    for one in outs:
        one.wait()


def per_device(*args):
    vmem, anywhere, smem = (
        pl.BlockSpec(memory_space=space) for space in (pltpu.VMEM, pl.ANY, pltpu.SMEM)
    )
    buf = pltpu.VMEM
    outs = pl.pallas_call(
        kernel,
        out_shape=(
            buf((TOK, KVH * GROUP * HD), BF16),
            buf((TOK, KVH * HD), BF16),
            buf((TOK, KVH * HD), BF16),
            buf((SHARD, KVH * HD), BF16),
            buf((SHARD, KVH * HD), BF16),
        ),
        in_specs=[anywhere, vmem, vmem, anywhere, anywhere, anywhere, smem, smem],
        out_specs=(anywhere,) * 5,
        scratch_shapes=[
            buf((TOK, KVH * NQ), BF16),
            buf((TOK, KVH * NQ), BF16),
            buf((TOK, KVH * NQ), BF16),
            buf((2, KVH, TOK, HD), BF16),
            buf((2, KVH, SHARD, HD), BF16),
            buf((KVH, NQ, HD), BF16),
            buf((KVH, NQ, HD), BF16),
            buf((KVH, ROOT, HD), BF16),
            buf((KVH, ROOT, HD), BF16),
            buf((KVH, ROOT, HD), BF16),
            buf((KVH, ROOT, HD), BF16),
            buf((KVH, 6, SHARD, HD), BF16),
            buf((KVH, SHARD, HD), BF16),
            buf((KVH, 4, SHARD, HD), BF16),
            buf((KVH, 2, HALF, HD), BF16),
            buf((KVH, 2, SHARD, HD), BF16),
            buf((KVH, 2, QUARTER, HD), BF16),
            buf((2, TOK, NQ), F32),
            buf((2, TOK, NQ), F32),
            buf((2, N_MEM, SHARD, NQ), F32),
            buf((2, N_MEM, SHARD, NQ), F32),
            buf((2, N_MEM + 1, NQ), F32),
            buf((2, 1, NQ), F32),
            buf((2, 1, NQ), F32),
            buf((HD, NQ), F32),
            buf((1, NQ), jnp.int32),
            buf((1, NQ), jnp.int32),
            pltpu.SemaphoreType.DMA((KVH, SLOTS)),
            pltpu.SemaphoreType.DMA((KVH, SLOTS)),
            pltpu.SemaphoreType.DMA((KVH, 9)),
        ],
        compiler_params=pltpu.CompilerParams(
            collective_id=0, has_side_effects=True, vmem_limit_bytes=60 * 2**20
        ),
        cost_estimate=pl.CostEstimate(
            flops=12 * 10**9, bytes_accessed=6 * 10**6, transcendentals=9 * 10**6
        ),
    )(*args)
    return pl.pallas_call(
        hand_over,
        out_shape=tuple(jax.ShapeDtypeStruct(out.shape, out.dtype) for out in outs),
        in_specs=[anywhere] * 5,
        out_specs=(anywhere,) * 5,
        scratch_shapes=[pltpu.SemaphoreType.DMA((5,))],
    )(*[pltpu.with_memory_space_constraint(out, pltpu.VMEM) for out in outs])


def solution(mesh):
    spec = P(("grp", "mem"), None)
    return jax.shard_map(
        per_device,
        mesh=mesh,
        in_specs=(spec,) * 8,
        out_specs=(spec,) * 5,
        check_vma=False,
    )
```

```python
import functools
import math

import jax
import jax.numpy as jnp
from jax import lax
from jax.experimental import pallas as pl
from jax.experimental.pallas import tpu as pltpu
from jax.sharding import PartitionSpec as P

KVH = 4
GROUP = 8
HD = 128
TOK = 128
NQ = GROUP * TOK
SHARD = 256
MAIN = 160
SIDES = (16, 80)
REST = SHARD - MAIN
ROW_TILE = 16
N_MEM = 8
RING = 4
ROOT = SHARD * N_MEM
LT = 256
NEG = -1e30
SCALE = 1.0 / math.sqrt(HD)
C2 = SCALE / math.log(2.0)
SLOTS = 34
START, OWN, NEAR_A, NEAR_B, FAR_A, FAR_B, BACK_A, BACK_B, BACK_C, BACK_D, DONE = range(11)
PLAN = {
    (START, 0): [(1, 0), (0, 0), (3, 0), (1, 1), (2, 0), (0, 1), (5, 0), (4, 0), (6, 0)],
    (OWN, 0): [(2, 1), (3, 1), (4, 1)],
    (NEAR_A, 0): [(9, 0), (8, 0), (7, 0), (0, 2), (10, 0), (5, 1), (11, 0), (1, 2), (1, 3), (3, 2), (6, 1), (0, 3)],
    (NEAR_B, 0): [(7, 1), (2, 2)],
    (NEAR_B, 1): [(8, 1)],
    (FAR_B, 0): [(10, 1)],
    (BACK_B, 0): [(11, 1), (5, 2), (4, 2), (9, 1), (3, 3)],
    (BACK_C, 0): [(6, 2)],
    (BACK_D, 0): [(7, 2), (5, 3)],
    (NEAR_A, 2): [(2, 3), (4, 3)],
    (FAR_B, 1): [(10, 2), (12, 0), (11, 2), (9, 2), (8, 2)],
    (BACK_B, 1): [(6, 3), (16, 0)],
    (BACK_C, 1): [(7, 3), (13, 0)],
    (NEAR_A, 3): [(14, 0)],
    (FAR_B, 2): [(13, 1), (9, 3), (15, 1), (10, 3), (12, 1), (11, 3), (8, 3)],
    (BACK_B, 2): [(19, 0)],
    (BACK_C, 2): [(16, 1), (14, 1), (17, 0)],
    (DONE, 2): [(15, 0)],
    (FAR_B, 3): [(12, 2), (18, 1)],
    (BACK_B, 3): [(14, 2), (13, 2), (15, 2)],
    (BACK_C, 3): [(16, 2), (19, 1), (12, 3), (16, 3), (14, 3), (15, 3), (13, 3), (21, 0)],
    (BACK_D, 3): [(21, 1), (17, 2), (17, 1), (18, 0), (19, 2), (18, 2), (17, 3)],
    (DONE, 3): [(19, 3), (18, 3), (22, 3), (20, 2), (20, 1), (20, 0), (21, 2), (21, 3), (20, 3)],
}
F32 = jnp.float32
BF16 = jnp.bfloat16
NT = (((1,), (1,)), ((), ()))


def kernel(
    q_in, kb_in, vb_in, kr_in, vr_in, do_in, len_in, fork_in,
    dq_out, dkb_out, dvb_out, dkr_out, dvr_out,
    q_vm, do_vm,
    qs, gs, kbuf, vbuf, pk, pv, rk, rkx, rvx, rvh, rvf, rvq,
    exp_own, dp_own, exp_all, dp_all, maxes, total, corr, dq_acc, fork_row, start_row,
    ssem, rsem, lsem,
):
    me = lax.axis_index("mem")
    x, z = me // RING, me % RING
    xn = 1 - x
    zp, zm, z2 = (z + 1) % RING, (z + 3) % RING, (z + 2) % RING

    def at(xi, zi):
        return xi * RING + zi

    def rows(xi, zi, first=0, count=SHARD):
        return pl.ds(pl.multiple_of(at(xi, zi) * SHARD + first, ROW_TILE), count)

    def head_cols(h):
        return pl.ds(pl.multiple_of(h * HD, HD), HD)

    right, left, across = at(x, zp), at(x, zm), at(xn, z)

    def copy(h, slot):
        own_k, own_v = kr_in.at[:, head_cols(h)], vr_in.at[:, head_cols(h)]

        def kv(buf, xi, zi, first=0, count=SHARD):
            return buf.at[h, rows(xi, zi, first, count), :]

        def same(buf, xi, zi, to, first=0, count=SHARD):
            ref = kv(buf, xi, zi, first, count)
            return ref, ref, to

        src, dst, to = {
            0: lambda: (own_k, kv(kbuf, x, z), across),
            1: lambda: (own_k, kv(kbuf, x, z), right),
            2: lambda: (own_k, kv(kbuf, x, z), left),
            3: lambda: same(kbuf, xn, z, right),
            4: lambda: same(kbuf, xn, z, left),
            5: lambda: same(kbuf, x, zm, right),
            6: lambda: same(kbuf, xn, zp, left),
            7: lambda: (own_v, kv(vbuf, x, z), across),
            8: lambda: (own_v, kv(vbuf, x, z), right),
            9: lambda: (own_v, kv(vbuf, x, z), left),
            10: lambda: same(vbuf, x, zm, right, 0, MAIN),
            11: lambda: same(vbuf, x, zp, left, MAIN, REST),
            12: lambda: same(vbuf, x, zm, across),
            13: lambda: same(vbuf, x, zp, across),
            14: lambda: same(vbuf, x, z2, across, 0, MAIN),
            15: lambda: same(vbuf, xn, zm, right, MAIN, SIDES[0]),
            31: lambda: same(vbuf, xn, zp, left, MAIN + SIDES[0], SIDES[1]),
            16: lambda: (kv(pk, x, z2), rk.at[h, 0], right),
            17: lambda: (kv(pk, xn, z2), rk.at[h, 1], left),
            18: lambda: (kv(pk, xn, zp), rk.at[h, 2], right),
            19: lambda: (kv(pk, x, zm), rk.at[h, 3], left),
            20: lambda: (kv(pk, x, zp), rk.at[h, 4], right),
            21: lambda: (kv(pk, xn, zm), rk.at[h, 5], left),
            22: lambda: (kv(pk, xn, z), rkx.at[h], across),
            23: lambda: (kv(pv, xn, z2, 0, MAIN), rvx.at[h, 0, pl.ds(0, MAIN), :], across),
            32: lambda: (kv(pv, xn, z2, MAIN, SIDES[0]), rvq.at[h, pl.ds(0, SIDES[0]), :], right),
            33: lambda: (
                kv(pv, xn, z2, MAIN + SIDES[0], SIDES[1]),
                rvq.at[h, pl.ds(SIDES[0], SIDES[1]), :],
                left,
            ),
            24: lambda: (kv(pv, xn, zp), rvx.at[h, 1], across),
            25: lambda: (kv(pv, xn, zm), rvx.at[h, 2], across),
            26: lambda: (kv(pv, xn, z), rvx.at[h, 3], across),
            27: lambda: (kv(pv, x, z2, 0, MAIN), rvh.at[h, pl.ds(0, MAIN), :], right),
            28: lambda: (kv(pv, x, z2, MAIN, REST), rvh.at[h, pl.ds(MAIN, REST), :], left),
            29: lambda: (kv(pv, x, zp), rvf.at[h, 0], right),
            30: lambda: (kv(pv, x, zm), rvf.at[h, 1], left),
        }[slot]()
        return pltpu.make_async_remote_copy(
            src_ref=src, dst_ref=dst,
            send_sem=ssem.at[h, slot], recv_sem=rsem.at[h, slot],
            device_id={"mem": to}, device_id_type=pl.DeviceIdType.MESH,
        )

    def send(h, *slots):
        for slot in slots:
            copy(h, slot).start()

    def arrive(h, *slots):
        for slot in slots:
            copy(h, slot).wait_recv()

    def wide_cols(h):
        return pl.ds(pl.multiple_of(h * NQ, NQ), NQ)

    def local(h, which):
        thin, wide, own = head_cols(h), wide_cols(h), rows(x, z)
        src, dst = (
            (kr_in.at[:, thin], kbuf.at[h, own, :]),
            (vr_in.at[:, thin], vbuf.at[h, own, :]),
            (q_in.at[:, wide], q_vm.at[:, wide]),
            (do_in.at[:, wide], do_vm.at[:, wide]),
        )[which]
        return pltpu.make_async_copy(src, dst, lsem.at[h, which])

    def f32(ref):
        return ref.astype(F32)

    def plus(buf, h, here, *terms):
        total_here = f32(buf[h, here, :])
        for term in terms:
            total_here = total_here + f32(term)
        buf[h, here, :] = total_here.astype(BF16)

    def sent(h, *slots):
        for slot in slots:
            copy(h, slot).wait_send()

    def pass_on(h, waits, sends):
        arrive(h, *waits)
        send(h, *sends)

    def value_side(h, side):
        arrive(h, 32 + side)
        zi, first = ((zp, 0), (zm, SIDES[0]))[side]
        came = rvq[h, first : first + SIDES[side]]
        plus(pv, h, rows(xn, zi, MAIN + first, SIDES[side]), came)
        send(h, 24 + side)

    def value_half(h):
        arrive(h, 23)
        plus(pv, h, rows(x, z2, 0, MAIN), rvx[h, 0, :MAIN])
        send(h, 27)

    def key_side(h, side):
        arrive(h, 16 + side)
        plus(pk, h, (rows(x, zp), rows(xn, zm))[side], rk[h, side])
        send(h, 20 + side)

    def value_block(h, side):
        arrive(h, 24 + side, 27 + side)
        zi = (zp, zm)[side]
        both, alone = ((0, MAIN), (MAIN, REST))[:: 1 - 2 * side]
        for (first, count), twice in ((both, True), (alone, False)):
            came = [rvx[h, 1 + side, first : first + count]]
            if twice:
                came.append(rvh[h, first : first + count])
            plus(pv, h, rows(x, zi, first, count), *came)
        send(h, 29 + side)

    def key_across(h):
        arrive(h, 18, 21)
        plus(pk, h, rows(xn, z), rk[h, 2], rk[h, 5])
        send(h, 22)

    def value_out(h):
        arrive(h, 26, 29, 30)
        dvr_out[:, head_cols(h)] = (
            f32(pv[h, rows(x, z), :]) + f32(rvx[h, 3]) + f32(rvf[h, 0]) + f32(rvf[h, 1])
        ).astype(BF16)

    def key_out(h):
        arrive(h, 19, 20, 22)
        dkr_out[:, head_cols(h)] = (
            f32(pk[h, rows(x, z), :]) + f32(rk[h, 3]) + f32(rk[h, 4]) + f32(rkx[h])
        ).astype(BF16)

    steps = [
        lambda h: send(h, 0),
        lambda h: send(h, 8, 9),
        lambda h: send(h, 7),
        lambda h: send(h, 1, 2),
        lambda h: pass_on(h, (0,), (3, 4)),
        lambda h: pass_on(h, (8,), (12, 10)),
        lambda h: pass_on(h, (9,), (13, 11)),
        lambda h: pass_on(h, (1,), (5,)),
        lambda h: pass_on(h, (4,), (6,)),
        lambda h: pass_on(h, (10,), (14,)),
        lambda h: pass_on(h, (12,), (15,)),
        lambda h: pass_on(h, (13,), (31,)),
        lambda h: value_side(h, 0),
        lambda h: value_side(h, 1),
        value_half,
        lambda h: key_side(h, 0),
        lambda h: key_side(h, 1),
        lambda h: value_block(h, 0),
        lambda h: value_block(h, 1),
        key_across,
        value_out,
        key_out,
        lambda h: late(),
    ]

    def late():
        back = (*range(16, 31), 32, 33)
        for h in range(KVH):
            sent(h, *(slot for slot in back if h < KVH - 1 or slot not in (22, 29, 30)))

    def run(piece, head):
        for number, h in PLAN.get((piece, head), ()):
            steps[number](h)

    def run_when(piece, head, guard=None):
        for h in range(KVH):
            if (piece, h) in PLAN:

                @pl.when(head == h if guard is None else (head == h) & guard)
                def _():
                    run(piece, h)

    barrier = pltpu.get_barrier_semaphore()
    for peer in (right, left, across):
        pl.semaphore_signal(
            barrier, inc=1, device_id={"mem": peer}, device_id_type=pl.DeviceIdType.MESH
        )
    for h in range(KVH):
        for which in range(4):
            local(h, which).start()
    lens = [len_in[0, b] for b in range(4)]
    ends = [lens[0], lens[0] + lens[1], lens[0] + lens[1] + lens[2]]
    place = lax.broadcasted_iota(jnp.int32, (1, NQ), 1) % TOK
    fork = jnp.full((1, NQ), fork_in[0, 0], jnp.int32)
    start = jnp.zeros((1, NQ), jnp.int32)
    for b, end in enumerate(ends):
        fork = jnp.where(place >= end, fork_in[0, b + 1], fork)
        start = jnp.where(place >= end, end, start)
    fork_row[...] = fork
    start_row[...] = start

    def lay_out(h):
        local(h, 2).wait()
        local(h, 3).wait()
        for g in range(GROUP):
            cols = pl.ds(pl.multiple_of((h * GROUP + g) * HD, HD), HD)
            qs[h, g * TOK : (g + 1) * TOK, :] = q_vm[:, cols]
            gs[h, g * TOK : (g + 1) * TOK, :] = do_vm[:, cols]

    lay_out(0)
    for h in range(KVH):
        local(h, 0).wait()
        local(h, 1).wait()
    pl.semaphore_wait(barrier, 3)
    run(START, 0)

    order = [
        (x, z), (xn, z), (x, zp), (x, zm), (xn, zp), (xn, zm), (x, z2), (xn, z2),
    ]

    def scores(key, h, lanes):
        return lax.dot_general(key, qs[h, lanes, :], NT, preferred_element_type=F32)

    def grads(value, h, lanes):
        return lax.dot_general(value, gs[h, lanes, :], NT, preferred_element_type=F32)

    lane_tiles = [slice(t, t + LT) for t in range(0, NQ, LT)]

    def first_own(h, par):
        key, value = kb_in[:, head_cols(h)], vb_in[:, head_cols(h)]
        for lanes in lane_tiles:
            row = lax.broadcasted_iota(jnp.int32, (TOK, LT), 0)
            lane = lax.broadcasted_iota(jnp.int32, (TOK, LT), 1) % TOK
            seen = (row <= lane) & (row >= start_row[:, lanes])
            s = jnp.where(seen, scores(key, h, lanes), NEG)
            top = jnp.max(s, axis=0, keepdims=True)
            e = jnp.exp2(s * C2 - top * C2)
            dp = grads(value, h, lanes)
            total[par, :, lanes] = jnp.sum(e, axis=0, keepdims=True)
            corr[par, :, lanes] = jnp.sum(e * dp, axis=0, keepdims=True)
            exp_own[par, :, lanes] = e
            dp_own[par, :, lanes] = dp
            maxes[par, 0:1, lanes] = top

    def first_root(h, par, i, shard):
        here = pl.ds(pl.multiple_of(shard * SHARD, SHARD), SHARD)
        key, value = kbuf[h, here, :], vbuf[h, here, :]
        base = shard * SHARD
        for lanes in lane_tiles:
            row = lax.broadcasted_iota(jnp.int32, (SHARD, LT), 0)
            s = jnp.where(row < fork_row[:, lanes] - base, scores(key, h, lanes), NEG)
            before = maxes[par, pl.ds(i, 1), lanes]
            top = jnp.maximum(before, jnp.max(s, axis=0, keepdims=True))
            shrink = jnp.exp2((before - top) * C2)
            e = jnp.exp2(s * C2 - top * C2)
            dp = grads(value, h, lanes)
            total[par, :, lanes] = total[par, :, lanes] * shrink + jnp.sum(e, axis=0, keepdims=True)
            corr[par, :, lanes] = corr[par, :, lanes] * shrink + jnp.sum(e * dp, axis=0, keepdims=True)
            exp_all[par, i, :, lanes] = e
            dp_all[par, i, :, lanes] = dp
            maxes[par, pl.ds(i + 1, 1), lanes] = top

    def second(h, par, key, e_ref, dp_ref, i):
        turned = key.T
        count = key.shape[0]
        dk = jnp.zeros((count, HD), F32)
        dv = jnp.zeros((count, HD), F32)
        for lanes in lane_tiles:
            p = e_ref[:, lanes] * maxes[par, pl.ds(i, 1), lanes]
            ds = (p * (dp_ref[:, lanes] - corr[par, :, lanes])).astype(BF16)
            dk += jnp.dot(ds, qs[h, lanes, :], preferred_element_type=F32)
            dv += jnp.dot(p.astype(BF16), gs[h, lanes, :], preferred_element_type=F32)
            dq_acc[:, lanes] += jnp.dot(turned, ds, preferred_element_type=F32)
        return (dk * SCALE).astype(BF16), dv.astype(BF16)

    def second_root(h, par, i, shard):
        here = pl.ds(pl.multiple_of(shard * SHARD, SHARD), SHARD)
        dk, dv = second(h, par, kbuf[h, here, :], exp_all.at[par, i], dp_all.at[par, i], i + 1)
        pk[h, here, :] = dk
        pv[h, here, :] = dv

    def when(condition, step, *args):
        @pl.when(condition)
        def _():
            step(*args)

    shards = [at(xi, zi) for xi, zi in order]

    def step(s, carry):
        now, after = s - 1, s
        odd = s % 2
        even = 1 - odd

        @pl.when(s < KVH)
        def _():
            first_own(after, odd)

        @pl.when(s < KVH - 1)
        def _():
            lay_out(s + 1)

        run_when(OWN, s)

        def first_group(far, carry):
            h = s - far
            par = (odd + far) % 2
            when(far == 0, arrive, h, 7)
            when(far == 1, arrive, h, 3)
            for c in range(4):
                if c == 2:

                    run_when(NEAR_A, h, far == 0)
                    run_when(FAR_A, h, far == 1)
                    when(far == 0, arrive, h, 2)
                    when(far == 1, arrive, h, 5, 11, 6, 14, 15, 31)
                first_root(h, par, far * 4 + c, jnp.where(far == 0, shards[c], shards[4 + c]))
            run_when(NEAR_B, h, far == 0)
            run_when(FAR_B, h, far == 1)
            return carry

        lax.fori_loop(jnp.where(s == KVH, 1, 0), jnp.where(s == 0, 1, 2), first_group, 0)

        def second_half():
            h = now
            inverse = 1.0 / total[even]
            maxes[even] = jnp.exp2((maxes[even] - maxes[even, N_MEM : N_MEM + 1, :]) * C2) * inverse
            corr[even] = corr[even] * inverse
            dq_acc[...] = jnp.zeros((HD, NQ), F32)

            def second_group(near, carry):
                for c, (i, j) in enumerate(((7, 2), (6, 3), (4, 1), (5, 0))):
                    second_root(
                        h, even, jnp.where(near == 0, i, j),
                        jnp.where(near == 0, shards[i], shards[j]),
                    )
                    if c == 1:
                        when(near == 0, send, h, 23, 17, 16, 32, 33, 28)
                        when(near == 1, send, h, 19)

                        run_when(BACK_A, h, near == 0)
                        run_when(BACK_C, h, near == 1)
                when(near == 0, send, h, 18)
                when(near == 1, send, h, 26)
                run_when(BACK_B, h, near == 0)
                run_when(BACK_D, h, near == 1)
                return carry

            lax.fori_loop(0, 2, second_group, 0)
            dk, dv = second(h, even, kb_in[:, head_cols(h)], exp_own.at[even], dp_own.at[even], 0)
            dkb_out[:, head_cols(h)] = dk
            dvb_out[:, head_cols(h)] = dv
            for g in range(GROUP):
                cols = pl.ds(pl.multiple_of((h * GROUP + g) * HD, HD), HD)
                dq_out[:, cols] = (dq_acc[:, g * TOK : (g + 1) * TOK].T * SCALE).astype(BF16)
            sent(h, *range(16), 31)
            run_when(DONE, h)

        when(s > 0, second_half)
        return carry

    lax.fori_loop(0, KVH + 1, step, 0)

    sent(KVH - 1, 22, 29, 30)


def hand_over(dq, dkb, dvb, dkr, dvr, dq_out, dkb_out, dvb_out, dkr_out, dvr_out, gone):
    srcs, dsts = (dq, dkb, dvb, dkr, dvr), (dq_out, dkb_out, dvb_out, dkr_out, dvr_out)
    outs = [pltpu.make_async_copy(a, b, gone.at[i]) for i, (a, b) in enumerate(zip(srcs, dsts))]
    for one in outs:
        one.start()
    for one in outs:
        one.wait()


def per_device(*args):
    vmem, anywhere, smem = (
        pl.BlockSpec(memory_space=space) for space in (pltpu.VMEM, pl.ANY, pltpu.SMEM)
    )
    buf = pltpu.VMEM
    outs = pl.pallas_call(
        kernel,
        out_shape=(
            buf((TOK, KVH * GROUP * HD), BF16),
            buf((TOK, KVH * HD), BF16),
            buf((TOK, KVH * HD), BF16),
            buf((SHARD, KVH * HD), BF16),
            buf((SHARD, KVH * HD), BF16),
        ),
        in_specs=[anywhere, vmem, vmem, anywhere, anywhere, anywhere, smem, smem],
        out_specs=(vmem,) * 5,
        scratch_shapes=[
            buf((TOK, KVH * NQ), BF16),
            buf((TOK, KVH * NQ), BF16),
            buf((KVH, NQ, HD), BF16),
            buf((KVH, NQ, HD), BF16),
            buf((KVH, ROOT, HD), BF16),
            buf((KVH, ROOT, HD), BF16),
            buf((KVH, ROOT, HD), BF16),
            buf((KVH, ROOT, HD), BF16),
            buf((KVH, 6, SHARD, HD), BF16),
            buf((KVH, SHARD, HD), BF16),
            buf((KVH, 4, SHARD, HD), BF16),
            buf((KVH, SHARD, HD), BF16),
            buf((KVH, 2, SHARD, HD), BF16),
            buf((KVH, REST, HD), BF16),
            buf((2, TOK, NQ), F32),
            buf((2, TOK, NQ), F32),
            buf((2, N_MEM, SHARD, NQ), F32),
            buf((2, N_MEM, SHARD, NQ), F32),
            buf((2, N_MEM + 1, NQ), F32),
            buf((2, 1, NQ), F32),
            buf((2, 1, NQ), F32),
            buf((HD, NQ), F32),
            buf((1, NQ), jnp.int32),
            buf((1, NQ), jnp.int32),
            pltpu.SemaphoreType.DMA((KVH, SLOTS)),
            pltpu.SemaphoreType.DMA((KVH, SLOTS)),
            pltpu.SemaphoreType.DMA((KVH, 4)),
        ],
        compiler_params=pltpu.CompilerParams(
            collective_id=0, has_side_effects=True, vmem_limit_bytes=60 * 2**20
        ),
        cost_estimate=pl.CostEstimate(
            flops=12 * 10**9, bytes_accessed=6 * 10**6, transcendentals=9 * 10**6
        ),
    )(*args)
    return pl.pallas_call(
        hand_over,
        out_shape=tuple(jax.ShapeDtypeStruct(out.shape, out.dtype) for out in outs),
        in_specs=[anywhere] * 5,
        out_specs=(anywhere,) * 5,
        scratch_shapes=[pltpu.SemaphoreType.DMA((5,))],
    )(*[pltpu.with_memory_space_constraint(out, pltpu.VMEM) for out in outs])


def solution(mesh):
    spec = P(("grp", "mem"), None)
    return jax.shard_map(
        per_device,
        mesh=mesh,
        in_specs=(spec,) * 8,
        out_specs=(spec,) * 5,
        check_vma=False,
    )
```

```python
import functools
import math

import jax
import jax.numpy as jnp
from jax import lax
from jax.experimental import pallas as pl
from jax.experimental.pallas import tpu as pltpu
from jax.sharding import PartitionSpec as P

KVH = 4
GROUP = 8
HD = 128
TOK = 128
NQ = GROUP * TOK
SHARD = 256
MAIN = 160
SIDES = (16, 80)
REST = SHARD - MAIN
ROW_TILE = 16
N_MEM = 8
RING = 4
ROOT = SHARD * N_MEM
LT = 256
NEG = -1e30
SCALE = 1.0 / math.sqrt(HD)
C2 = SCALE / math.log(2.0)
SLOTS = 34
FORWARD = 4
START, OWN, NEAR_A, NEAR_B, FAR_A, FAR_B, BACK_A, BACK_B, BACK_C, BACK_D, DONE = range(11)
PLAN = {
    (START, 0): [(1, 0), (0, 0), (3, 0), (1, 1), (2, 0), (0, 1), (5, 0), (4, 0), (6, 0)],
    (OWN, 0): [(2, 1), (3, 1), (4, 1)],
    (NEAR_A, 0): [(9, 0), (8, 0), (7, 0), (0, 2), (10, 0), (5, 1), (11, 0), (1, 2), (1, 3), (3, 2), (6, 1), (0, 3)],
    (NEAR_B, 0): [(7, 1), (2, 2)],
    (NEAR_B, 1): [(8, 1)],
    (FAR_B, 0): [(10, 1)],
    (BACK_B, 0): [(11, 1), (5, 2), (4, 2), (9, 1), (3, 3)],
    (BACK_C, 0): [(6, 2)],
    (BACK_D, 0): [(7, 2), (5, 3)],
    (NEAR_A, 2): [(2, 3), (4, 3)],
    (FAR_B, 1): [(10, 2), (12, 0), (11, 2), (9, 2), (8, 2)],
    (BACK_B, 1): [(6, 3), (16, 0)],
    (BACK_C, 1): [(7, 3), (13, 0)],
    (NEAR_A, 3): [(14, 0)],
    (FAR_B, 2): [(13, 1), (9, 3), (15, 1), (10, 3), (12, 1), (11, 3), (8, 3)],
    (BACK_B, 2): [(19, 0)],
    (BACK_C, 2): [(16, 1), (14, 1), (17, 0)],
    (DONE, 2): [(15, 0)],
    (FAR_B, 3): [(12, 2), (18, 1)],
    (BACK_B, 3): [(14, 2), (13, 2), (15, 2)],
    (BACK_C, 3): [(16, 2), (19, 1), (12, 3), (16, 3), (14, 3), (15, 3), (13, 3), (21, 0)],
    (BACK_D, 3): [(21, 1), (17, 2), (17, 1), (18, 0), (19, 2), (18, 2), (17, 3)],
    (DONE, 3): [(19, 3), (18, 3), (22, 3), (20, 2), (20, 1), (20, 0), (21, 2), (21, 3), (20, 3)],
}
F32 = jnp.float32
BF16 = jnp.bfloat16
NT = (((1,), (1,)), ((), ()))


def kernel(
    q_in, kb_hbm, vb_hbm, kr_in, vr_in, do_in, len_hbm, fork_hbm,
    dq_out, dkb_out, dvb_out, dkr_out, dvr_out,
    q_vm, do_vm, kb_in, vb_in, len_in, fork_in,
    qs, gs, kbuf, vbuf, pk, pv, rk, rkx, rvx, rvh, rvf, rvq,
    exp_own, dp_own, exp_all, dp_all, maxes, total, corr, dq_acc, fork_row, start_row,
    ssem, rsem, lsem, isem,
):
    me = lax.axis_index("mem")
    x, z = me // RING, me % RING
    xn = 1 - x
    zp, zm, z2 = (z + 1) % RING, (z + 3) % RING, (z + 2) % RING

    def at(xi, zi):
        return xi * RING + zi

    def rows(xi, zi, first=0, count=SHARD):
        return pl.ds(pl.multiple_of(at(xi, zi) * SHARD + first, ROW_TILE), count)

    def head_cols(h):
        return pl.ds(pl.multiple_of(h * HD, HD), HD)

    right, left, across = at(x, zp), at(x, zm), at(xn, z)

    def copy(h, slot):
        own_k, own_v = kr_in.at[:, head_cols(h)], vr_in.at[:, head_cols(h)]

        def kv(buf, xi, zi, first=0, count=SHARD):
            return buf.at[h, rows(xi, zi, first, count), :]

        def same(buf, xi, zi, to, first=0, count=SHARD):
            ref = kv(buf, xi, zi, first, count)
            return ref, ref, to

        src, dst, to = {
            0: lambda: (own_k, kv(kbuf, x, z), across),
            1: lambda: (own_k, kv(kbuf, x, z), right),
            2: lambda: (own_k, kv(kbuf, x, z), left),
            3: lambda: same(kbuf, xn, z, right),
            4: lambda: same(kbuf, xn, z, left),
            5: lambda: same(kbuf, x, zm, right),
            6: lambda: same(kbuf, xn, zp, left),
            7: lambda: (own_v, kv(vbuf, x, z), across),
            8: lambda: (own_v, kv(vbuf, x, z), right),
            9: lambda: (own_v, kv(vbuf, x, z), left),
            10: lambda: same(vbuf, x, zm, right, 0, MAIN),
            11: lambda: same(vbuf, x, zp, left, MAIN, REST),
            12: lambda: same(vbuf, x, zm, across),
            13: lambda: same(vbuf, x, zp, across),
            14: lambda: same(vbuf, x, z2, across, 0, MAIN),
            15: lambda: same(vbuf, xn, zm, right, MAIN, SIDES[0]),
            31: lambda: same(vbuf, xn, zp, left, MAIN + SIDES[0], SIDES[1]),
            16: lambda: (kv(pk, x, z2), rk.at[h, 0], right),
            17: lambda: (kv(pk, xn, z2), rk.at[h, 1], left),
            18: lambda: (kv(pk, xn, zp), rk.at[h, 2], right),
            19: lambda: (kv(pk, x, zm), rk.at[h, 3], left),
            20: lambda: (kv(pk, x, zp), rk.at[h, 4], right),
            21: lambda: (kv(pk, xn, zm), rk.at[h, 5], left),
            22: lambda: (kv(pk, xn, z), rkx.at[h], across),
            23: lambda: (kv(pv, xn, z2, 0, MAIN), rvx.at[h, 0, pl.ds(0, MAIN), :], across),
            32: lambda: (kv(pv, xn, z2, MAIN, SIDES[0]), rvq.at[h, pl.ds(0, SIDES[0]), :], right),
            33: lambda: (
                kv(pv, xn, z2, MAIN + SIDES[0], SIDES[1]),
                rvq.at[h, pl.ds(SIDES[0], SIDES[1]), :],
                left,
            ),
            24: lambda: (kv(pv, xn, zp), rvx.at[h, 1], across),
            25: lambda: (kv(pv, xn, zm), rvx.at[h, 2], across),
            26: lambda: (kv(pv, xn, z), rvx.at[h, 3], across),
            27: lambda: (kv(pv, x, z2, 0, MAIN), rvh.at[h, pl.ds(0, MAIN), :], right),
            28: lambda: (kv(pv, x, z2, MAIN, REST), rvh.at[h, pl.ds(MAIN, REST), :], left),
            29: lambda: (kv(pv, x, zp), rvf.at[h, 0], right),
            30: lambda: (kv(pv, x, zm), rvf.at[h, 1], left),
        }[slot]()
        return pltpu.make_async_remote_copy(
            src_ref=src, dst_ref=dst,
            send_sem=ssem.at[h, slot], recv_sem=rsem.at[h, slot],
            device_id={"mem": to}, device_id_type=pl.DeviceIdType.MESH,
        )

    def send(h, *slots):
        for slot in slots:
            copy(h, slot).start()

    def arrive(h, *slots):
        for slot in slots:
            copy(h, slot).wait_recv()

    def wide_cols(h):
        return pl.ds(pl.multiple_of(h * NQ, NQ), NQ)

    def local(h, which):
        thin, wide, own = head_cols(h), wide_cols(h), rows(x, z)
        src, dst = (
            (kr_in.at[:, thin], kbuf.at[h, own, :]),
            (vr_in.at[:, thin], vbuf.at[h, own, :]),
            (q_in.at[:, wide], q_vm.at[:, wide]),
            (do_in.at[:, wide], do_vm.at[:, wide]),
        )[which]
        return pltpu.make_async_copy(src, dst, lsem.at[h, which])

    def f32(ref):
        return ref.astype(F32)

    def plus(buf, h, here, *terms):
        total_here = f32(buf[h, here, :])
        for term in terms:
            total_here = total_here + f32(term)
        buf[h, here, :] = total_here.astype(BF16)

    def sent(h, *slots):
        for slot in slots:
            copy(h, slot).wait_send()

    def pass_on(h, waits, sends):
        arrive(h, *waits)
        send(h, *sends)

    def value_side(h, side):
        arrive(h, 32 + side)
        zi, first = ((zp, 0), (zm, SIDES[0]))[side]
        came = rvq[h, first : first + SIDES[side]]
        plus(pv, h, rows(xn, zi, MAIN + first, SIDES[side]), came)
        send(h, 24 + side)

    def value_half(h):
        arrive(h, 23)
        plus(pv, h, rows(x, z2, 0, MAIN), rvx[h, 0, :MAIN])
        send(h, 27)

    def key_side(h, side):
        arrive(h, 16 + side)
        plus(pk, h, (rows(x, zp), rows(xn, zm))[side], rk[h, side])
        send(h, 20 + side)

    def value_block(h, side):
        arrive(h, 24 + side, 27 + side)
        zi = (zp, zm)[side]
        both, alone = ((0, MAIN), (MAIN, REST))[:: 1 - 2 * side]
        for (first, count), twice in ((both, True), (alone, False)):
            came = [rvx[h, 1 + side, first : first + count]]
            if twice:
                came.append(rvh[h, first : first + count])
            plus(pv, h, rows(x, zi, first, count), *came)
        send(h, 29 + side)

    def key_across(h):
        arrive(h, 18, 21)
        plus(pk, h, rows(xn, z), rk[h, 2], rk[h, 5])
        send(h, 22)

    def value_out(h):
        arrive(h, 26, 29, 30)
        dvr_out[:, head_cols(h)] = (
            f32(pv[h, rows(x, z), :]) + f32(rvx[h, 3]) + f32(rvf[h, 0]) + f32(rvf[h, 1])
        ).astype(BF16)

    def key_out(h):
        arrive(h, 19, 20, 22)
        dkr_out[:, head_cols(h)] = (
            f32(pk[h, rows(x, z), :]) + f32(rk[h, 3]) + f32(rk[h, 4]) + f32(rkx[h])
        ).astype(BF16)

    steps = [
        lambda h: send(h, 0),
        lambda h: send(h, 8, 9),
        lambda h: send(h, 7),
        lambda h: send(h, 1, 2),
        lambda h: pass_on(h, (0,), (3, 4)),
        lambda h: pass_on(h, (8,), (12, 10)),
        lambda h: pass_on(h, (9,), (13, 11)),
        lambda h: pass_on(h, (1,), (5,)),
        lambda h: pass_on(h, (4,), (6,)),
        lambda h: pass_on(h, (10,), (14,)),
        lambda h: pass_on(h, (12,), (15,)),
        lambda h: pass_on(h, (13,), (31,)),
        lambda h: value_side(h, 0),
        lambda h: value_side(h, 1),
        value_half,
        lambda h: key_side(h, 0),
        lambda h: key_side(h, 1),
        lambda h: value_block(h, 0),
        lambda h: value_block(h, 1),
        key_across,
        value_out,
        key_out,
        lambda h: late(),
    ]

    def late():
        back = (*range(16, 31), 32, 33)
        for h in range(KVH):
            sent(h, *(slot for slot in back if h < KVH - 1 or slot not in (22, 29, 30)))

    def run(piece, head):
        for number, h in PLAN.get((piece, head), ()):
            steps[number](h)

    def run_when(piece, head, guard=None):
        for h in range(KVH):
            if (piece, h) in PLAN:

                @pl.when(head == h if guard is None else (head == h) & guard)
                def _():
                    run(piece, h)

    barrier = pltpu.get_barrier_semaphore()
    for peer in (right, left, across):
        pl.semaphore_signal(
            barrier, inc=1, device_id={"mem": peer}, device_id_type=pl.DeviceIdType.MESH
        )
    pl.semaphore_wait(barrier, 3)
    for number, h in PLAN[START, 0]:
        if number < FORWARD:
            steps[number](h)
    small = [
        pltpu.make_async_copy(src, dst, isem.at[i])
        for i, (src, dst) in enumerate(
            ((len_hbm, len_in), (fork_hbm, fork_in), (kb_hbm, kb_in), (vb_hbm, vb_in))
        )
    ]
    for one in small:
        one.start()
    for h in range(KVH):
        for which in range(4):
            local(h, which).start()
    for one in small:
        one.wait()

    lens = [len_in[0, b] for b in range(4)]
    ends = [lens[0], lens[0] + lens[1], lens[0] + lens[1] + lens[2]]
    place = lax.broadcasted_iota(jnp.int32, (1, NQ), 1) % TOK
    fork = jnp.full((1, NQ), fork_in[0, 0], jnp.int32)
    start = jnp.zeros((1, NQ), jnp.int32)
    for b, end in enumerate(ends):
        fork = jnp.where(place >= end, fork_in[0, b + 1], fork)
        start = jnp.where(place >= end, end, start)
    fork_row[...] = fork
    start_row[...] = start

    def lay_out(h):
        local(h, 2).wait()
        local(h, 3).wait()
        for g in range(GROUP):
            cols = pl.ds(pl.multiple_of((h * GROUP + g) * HD, HD), HD)
            qs[h, g * TOK : (g + 1) * TOK, :] = q_vm[:, cols]
            gs[h, g * TOK : (g + 1) * TOK, :] = do_vm[:, cols]

    lay_out(0)
    for h in range(KVH):
        local(h, 0).wait()
        local(h, 1).wait()
    for number, h in PLAN[START, 0]:
        if number >= FORWARD:
            steps[number](h)

    order = [
        (x, z), (xn, z), (x, zp), (x, zm), (xn, zp), (xn, zm), (x, z2), (xn, z2),
    ]

    def scores(key, h, lanes):
        return lax.dot_general(key, qs[h, lanes, :], NT, preferred_element_type=F32)

    def grads(value, h, lanes):
        return lax.dot_general(value, gs[h, lanes, :], NT, preferred_element_type=F32)

    lane_tiles = [slice(t, t + LT) for t in range(0, NQ, LT)]

    def first_own(h, par):
        key, value = kb_in[:, head_cols(h)], vb_in[:, head_cols(h)]
        for lanes in lane_tiles:
            row = lax.broadcasted_iota(jnp.int32, (TOK, LT), 0)
            lane = lax.broadcasted_iota(jnp.int32, (TOK, LT), 1) % TOK
            seen = (row <= lane) & (row >= start_row[:, lanes])
            s = jnp.where(seen, scores(key, h, lanes), NEG)
            top = jnp.max(s, axis=0, keepdims=True)
            e = jnp.exp2(s * C2 - top * C2)
            dp = grads(value, h, lanes)
            total[par, :, lanes] = jnp.sum(e, axis=0, keepdims=True)
            corr[par, :, lanes] = jnp.sum(e * dp, axis=0, keepdims=True)
            exp_own[par, :, lanes] = e
            dp_own[par, :, lanes] = dp
            maxes[par, 0:1, lanes] = top

    def first_root(h, par, i, shard):
        here = pl.ds(pl.multiple_of(shard * SHARD, SHARD), SHARD)
        key, value = kbuf[h, here, :], vbuf[h, here, :]
        base = shard * SHARD
        for lanes in lane_tiles:
            row = lax.broadcasted_iota(jnp.int32, (SHARD, LT), 0)
            s = jnp.where(row < fork_row[:, lanes] - base, scores(key, h, lanes), NEG)
            before = maxes[par, pl.ds(i, 1), lanes]
            top = jnp.maximum(before, jnp.max(s, axis=0, keepdims=True))
            shrink = jnp.exp2((before - top) * C2)
            e = jnp.exp2(s * C2 - top * C2)
            dp = grads(value, h, lanes)
            total[par, :, lanes] = total[par, :, lanes] * shrink + jnp.sum(e, axis=0, keepdims=True)
            corr[par, :, lanes] = corr[par, :, lanes] * shrink + jnp.sum(e * dp, axis=0, keepdims=True)
            exp_all[par, i, :, lanes] = e
            dp_all[par, i, :, lanes] = dp
            maxes[par, pl.ds(i + 1, 1), lanes] = top

    def second(h, par, key, e_ref, dp_ref, i):
        turned = key.T
        count = key.shape[0]
        dk = jnp.zeros((count, HD), F32)
        dv = jnp.zeros((count, HD), F32)
        for lanes in lane_tiles:
            p = e_ref[:, lanes] * maxes[par, pl.ds(i, 1), lanes]
            ds = (p * (dp_ref[:, lanes] - corr[par, :, lanes])).astype(BF16)
            dk += jnp.dot(ds, qs[h, lanes, :], preferred_element_type=F32)
            dv += jnp.dot(p.astype(BF16), gs[h, lanes, :], preferred_element_type=F32)
            dq_acc[:, lanes] += jnp.dot(turned, ds, preferred_element_type=F32)
        return (dk * SCALE).astype(BF16), dv.astype(BF16)

    def second_root(h, par, i, shard):
        here = pl.ds(pl.multiple_of(shard * SHARD, SHARD), SHARD)
        dk, dv = second(h, par, kbuf[h, here, :], exp_all.at[par, i], dp_all.at[par, i], i + 1)
        pk[h, here, :] = dk
        pv[h, here, :] = dv

    def when(condition, step, *args):
        @pl.when(condition)
        def _():
            step(*args)

    shards = [at(xi, zi) for xi, zi in order]

    def step(s, carry):
        now, after = s - 1, s
        odd = s % 2
        even = 1 - odd

        @pl.when(s < KVH)
        def _():
            first_own(after, odd)

        @pl.when(s < KVH - 1)
        def _():
            lay_out(s + 1)

        run_when(OWN, s)

        def first_group(far, carry):
            h = s - far
            par = (odd + far) % 2
            when(far == 0, arrive, h, 7)
            when(far == 1, arrive, h, 3)
            for c in range(4):
                if c == 2:

                    run_when(NEAR_A, h, far == 0)
                    run_when(FAR_A, h, far == 1)
                    when(far == 0, arrive, h, 2)
                    when(far == 1, arrive, h, 5, 11, 6, 14, 15, 31)
                first_root(h, par, far * 4 + c, jnp.where(far == 0, shards[c], shards[4 + c]))
            run_when(NEAR_B, h, far == 0)
            run_when(FAR_B, h, far == 1)
            return carry

        lax.fori_loop(jnp.where(s == KVH, 1, 0), jnp.where(s == 0, 1, 2), first_group, 0)

        def second_half():
            h = now
            inverse = 1.0 / total[even]
            maxes[even] = jnp.exp2((maxes[even] - maxes[even, N_MEM : N_MEM + 1, :]) * C2) * inverse
            corr[even] = corr[even] * inverse
            dq_acc[...] = jnp.zeros((HD, NQ), F32)

            def second_group(near, carry):
                for c, (i, j) in enumerate(((7, 2), (6, 3), (4, 1), (5, 0))):
                    second_root(
                        h, even, jnp.where(near == 0, i, j),
                        jnp.where(near == 0, shards[i], shards[j]),
                    )
                    if c == 1:
                        when(near == 0, send, h, 23, 17, 16, 32, 33, 28)
                        when(near == 1, send, h, 19)

                        run_when(BACK_A, h, near == 0)
                        run_when(BACK_C, h, near == 1)
                when(near == 0, send, h, 18)
                when(near == 1, send, h, 26)
                run_when(BACK_B, h, near == 0)
                run_when(BACK_D, h, near == 1)
                return carry

            lax.fori_loop(0, 2, second_group, 0)
            dk, dv = second(h, even, kb_in[:, head_cols(h)], exp_own.at[even], dp_own.at[even], 0)
            dkb_out[:, head_cols(h)] = dk
            dvb_out[:, head_cols(h)] = dv
            for g in range(GROUP):
                cols = pl.ds(pl.multiple_of((h * GROUP + g) * HD, HD), HD)
                dq_out[:, cols] = (dq_acc[:, g * TOK : (g + 1) * TOK].T * SCALE).astype(BF16)
            sent(h, *range(16), 31)
            run_when(DONE, h)

        when(s > 0, second_half)
        return carry

    lax.fori_loop(0, KVH + 1, step, 0)

    sent(KVH - 1, 22, 29, 30)


def hand_over(dq, dkb, dvb, dkr, dvr, dq_out, dkb_out, dvb_out, dkr_out, dvr_out, gone):
    srcs, dsts = (dq, dkb, dvb, dkr, dvr), (dq_out, dkb_out, dvb_out, dkr_out, dvr_out)
    outs = [pltpu.make_async_copy(a, b, gone.at[i]) for i, (a, b) in enumerate(zip(srcs, dsts))]
    for one in outs:
        one.start()
    for one in outs:
        one.wait()


def per_device(*args):
    vmem, anywhere = (pl.BlockSpec(memory_space=space) for space in (pltpu.VMEM, pl.ANY))
    buf = pltpu.VMEM
    outs = pl.pallas_call(
        kernel,
        out_shape=(
            buf((TOK, KVH * GROUP * HD), BF16),
            buf((TOK, KVH * HD), BF16),
            buf((TOK, KVH * HD), BF16),
            buf((SHARD, KVH * HD), BF16),
            buf((SHARD, KVH * HD), BF16),
        ),
        in_specs=[anywhere] * 8,
        out_specs=(vmem,) * 5,
        scratch_shapes=[
            buf((TOK, KVH * NQ), BF16),
            buf((TOK, KVH * NQ), BF16),
            buf((TOK, KVH * HD), BF16),
            buf((TOK, KVH * HD), BF16),
            pltpu.SMEM((1, 4), jnp.int32),
            pltpu.SMEM((1, 4), jnp.int32),
            buf((KVH, NQ, HD), BF16),
            buf((KVH, NQ, HD), BF16),
            buf((KVH, ROOT, HD), BF16),
            buf((KVH, ROOT, HD), BF16),
            buf((KVH, ROOT, HD), BF16),
            buf((KVH, ROOT, HD), BF16),
            buf((KVH, 6, SHARD, HD), BF16),
            buf((KVH, SHARD, HD), BF16),
            buf((KVH, 4, SHARD, HD), BF16),
            buf((KVH, SHARD, HD), BF16),
            buf((KVH, 2, SHARD, HD), BF16),
            buf((KVH, REST, HD), BF16),
            buf((2, TOK, NQ), F32),
            buf((2, TOK, NQ), F32),
            buf((2, N_MEM, SHARD, NQ), F32),
            buf((2, N_MEM, SHARD, NQ), F32),
            buf((2, N_MEM + 1, NQ), F32),
            buf((2, 1, NQ), F32),
            buf((2, 1, NQ), F32),
            buf((HD, NQ), F32),
            buf((1, NQ), jnp.int32),
            buf((1, NQ), jnp.int32),
            pltpu.SemaphoreType.DMA((KVH, SLOTS)),
            pltpu.SemaphoreType.DMA((KVH, SLOTS)),
            pltpu.SemaphoreType.DMA((KVH, 4)),
            pltpu.SemaphoreType.DMA((4,)),
        ],
        compiler_params=pltpu.CompilerParams(
            collective_id=0, has_side_effects=True, vmem_limit_bytes=60 * 2**20
        ),
        cost_estimate=pl.CostEstimate(
            flops=12 * 10**9, bytes_accessed=6 * 10**6, transcendentals=9 * 10**6
        ),
    )(*args)
    return pl.pallas_call(
        hand_over,
        out_shape=tuple(jax.ShapeDtypeStruct(out.shape, out.dtype) for out in outs),
        in_specs=[anywhere] * 5,
        out_specs=(anywhere,) * 5,
        scratch_shapes=[pltpu.SemaphoreType.DMA((5,))],
    )(*[pltpu.with_memory_space_constraint(out, pltpu.VMEM) for out in outs])


def solution(mesh):
    spec = P(("grp", "mem"), None)
    return jax.shard_map(
        per_device,
        mesh=mesh,
        in_specs=(spec,) * 8,
        out_specs=(spec,) * 5,
        check_vma=False,
    )
```

```python
import functools
import math

import jax
import jax.numpy as jnp
from jax import lax
from jax.experimental import pallas as pl
from jax.experimental.pallas import tpu as pltpu
from jax.sharding import PartitionSpec as P

KVH = 4
GROUP = 8
HD = 128
TOK = 128
NQ = GROUP * TOK
SHARD = 256
MAIN = 160
SIDES = (16, 80)
REST = SHARD - MAIN
ROW_TILE = 16
N_MEM = 8
RING = 4
ROOT = SHARD * N_MEM
LT = 256
NEG = -1e30
SCALE = 1.0 / math.sqrt(HD)
C2 = SCALE / math.log(2.0)
SLOTS = 34
FORWARD = 4
START, OWN, NEAR_A, NEAR_B, FAR_A, FAR_B, BACK_A, BACK_B, BACK_C, BACK_D, DONE = range(11)
PLAN = {
    (START, 0): [(1, 0), (0, 0), (3, 0), (1, 1), (2, 0), (0, 1), (5, 0), (4, 0), (6, 0)],
    (OWN, 0): [(2, 1), (3, 1), (4, 1)],
    (NEAR_A, 0): [(9, 0), (8, 0), (7, 0), (0, 2), (10, 0), (5, 1), (11, 0), (1, 2), (1, 3), (3, 2), (6, 1), (0, 3)],
    (NEAR_B, 0): [(7, 1), (2, 2)],
    (NEAR_B, 1): [(8, 1)],
    (FAR_B, 0): [(10, 1)],
    (BACK_B, 0): [(11, 1), (5, 2), (4, 2), (9, 1), (3, 3)],
    (BACK_C, 0): [(6, 2)],
    (BACK_D, 0): [(7, 2), (5, 3)],
    (NEAR_A, 2): [(2, 3), (4, 3)],
    (FAR_B, 1): [(10, 2), (12, 0), (11, 2), (9, 2), (8, 2)],
    (BACK_B, 1): [(6, 3), (16, 0)],
    (BACK_C, 1): [(7, 3), (13, 0)],
    (NEAR_A, 3): [(14, 0)],
    (FAR_B, 2): [(13, 1), (9, 3), (15, 1), (10, 3), (12, 1), (11, 3), (8, 3)],
    (BACK_B, 2): [(19, 0)],
    (BACK_C, 2): [(16, 1), (14, 1), (17, 0)],
    (DONE, 2): [(15, 0)],
    (FAR_B, 3): [(12, 2), (18, 1)],
    (BACK_B, 3): [(14, 2), (13, 2), (15, 2)],
    (BACK_C, 3): [(16, 2), (19, 1), (12, 3), (16, 3), (14, 3), (15, 3), (13, 3), (21, 0)],
    (BACK_D, 3): [(21, 1), (17, 2), (17, 1), (18, 0), (19, 2), (18, 2), (17, 3)],
    (DONE, 3): [(19, 3), (18, 3), (22, 3), (20, 2), (20, 1), (20, 0), (21, 2), (21, 3), (20, 3)],
}
F32 = jnp.float32
BF16 = jnp.bfloat16
NT = (((1,), (1,)), ((), ()))


def kernel(
    q_in, kb_hbm, vb_hbm, kr_in, vr_in, do_in, len_hbm, fork_hbm,
    dq_out, dkb_out, dvb_out, dkr_out, dvr_out,
    q_vm, do_vm, kb_in, vb_in, len_in, fork_in,
    qs, gs, kbuf, vbuf, pk, pv, rk, rkx, rvx, rvh, rvf, rvq,
    exp_own, dp_own, exp_all, dp_all, maxes, total, corr, dq_acc, fork_row, start_row,
    ssem, rsem, lsem, isem,
):
    me = lax.axis_index("mem")
    x, z = me // RING, me % RING
    xn = 1 - x
    zp, zm, z2 = (z + 1) % RING, (z + 3) % RING, (z + 2) % RING

    def at(xi, zi):
        return xi * RING + zi

    def rows(xi, zi, first=0, count=SHARD):
        return pl.ds(pl.multiple_of(at(xi, zi) * SHARD + first, ROW_TILE), count)

    def head_cols(h):
        return pl.ds(pl.multiple_of(h * HD, HD), HD)

    right, left, across = at(x, zp), at(x, zm), at(xn, z)

    def copy(h, slot):
        own_k, own_v = kr_in.at[:, head_cols(h)], vr_in.at[:, head_cols(h)]

        def kv(buf, xi, zi, first=0, count=SHARD):
            return buf.at[h, rows(xi, zi, first, count), :]

        def same(buf, xi, zi, to, first=0, count=SHARD):
            ref = kv(buf, xi, zi, first, count)
            return ref, ref, to

        src, dst, to = {
            0: lambda: (own_k, kv(kbuf, x, z), across),
            1: lambda: (own_k, kv(kbuf, x, z), right),
            2: lambda: (own_k, kv(kbuf, x, z), left),
            3: lambda: same(kbuf, xn, z, right),
            4: lambda: same(kbuf, xn, z, left),
            5: lambda: same(kbuf, x, zm, right),
            6: lambda: same(kbuf, xn, zp, left),
            7: lambda: (own_v, kv(vbuf, x, z), across),
            8: lambda: (own_v, kv(vbuf, x, z), right),
            9: lambda: (own_v, kv(vbuf, x, z), left),
            10: lambda: same(vbuf, x, zm, right, 0, MAIN),
            11: lambda: same(vbuf, x, zp, left, MAIN, REST),
            12: lambda: same(vbuf, x, zm, across),
            13: lambda: same(vbuf, x, zp, across),
            14: lambda: same(vbuf, x, z2, across, 0, MAIN),
            15: lambda: same(vbuf, xn, zm, right, MAIN, SIDES[0]),
            31: lambda: same(vbuf, xn, zp, left, MAIN + SIDES[0], SIDES[1]),
            16: lambda: (kv(pk, x, z2), rk.at[h, 0], right),
            17: lambda: (kv(pk, xn, z2), rk.at[h, 1], left),
            18: lambda: (kv(pk, xn, zp), rk.at[h, 2], right),
            19: lambda: (kv(pk, x, zm), rk.at[h, 3], left),
            20: lambda: (kv(pk, x, zp), rk.at[h, 4], right),
            21: lambda: (kv(pk, xn, zm), rk.at[h, 5], left),
            22: lambda: (kv(pk, xn, z), rkx.at[h], across),
            23: lambda: (kv(pv, xn, z2, 0, MAIN), rvx.at[h, 0, pl.ds(0, MAIN), :], across),
            32: lambda: (kv(pv, xn, z2, MAIN, SIDES[0]), rvq.at[h, pl.ds(0, SIDES[0]), :], right),
            33: lambda: (
                kv(pv, xn, z2, MAIN + SIDES[0], SIDES[1]),
                rvq.at[h, pl.ds(SIDES[0], SIDES[1]), :],
                left,
            ),
            24: lambda: (kv(pv, xn, zp), rvx.at[h, 1], across),
            25: lambda: (kv(pv, xn, zm), rvx.at[h, 2], across),
            26: lambda: (kv(pv, xn, z), rvx.at[h, 3], across),
            27: lambda: (kv(pv, x, z2, 0, MAIN), rvh.at[h, pl.ds(0, MAIN), :], right),
            28: lambda: (kv(pv, x, z2, MAIN, REST), rvh.at[h, pl.ds(MAIN, REST), :], left),
            29: lambda: (kv(pv, x, zp), rvf.at[h, 0], right),
            30: lambda: (kv(pv, x, zm), rvf.at[h, 1], left),
        }[slot]()
        return pltpu.make_async_remote_copy(
            src_ref=src, dst_ref=dst,
            send_sem=ssem.at[h, slot], recv_sem=rsem.at[h, slot],
            device_id={"mem": to}, device_id_type=pl.DeviceIdType.MESH,
        )

    def send(h, *slots):
        for slot in slots:
            copy(h, slot).start()

    def arrive(h, *slots):
        for slot in slots:
            copy(h, slot).wait_recv()

    def wide_cols(h):
        return pl.ds(pl.multiple_of(h * NQ, NQ), NQ)

    def local(h, which):
        thin, wide, own = head_cols(h), wide_cols(h), rows(x, z)
        src, dst = (
            (kr_in.at[:, thin], kbuf.at[h, own, :]),
            (vr_in.at[:, thin], vbuf.at[h, own, :]),
            (q_in.at[:, wide], q_vm.at[:, wide]),
            (do_in.at[:, wide], do_vm.at[:, wide]),
        )[which]
        return pltpu.make_async_copy(src, dst, lsem.at[h, which])

    def f32(ref):
        return ref.astype(F32)

    def plus(buf, h, here, *terms):
        total_here = f32(buf[h, here, :])
        for term in terms:
            total_here = total_here + f32(term)
        buf[h, here, :] = total_here.astype(BF16)

    def sent(h, *slots):
        for slot in slots:
            copy(h, slot).wait_send()

    def pass_on(h, waits, sends):
        arrive(h, *waits)
        send(h, *sends)

    def value_side(h, side):
        arrive(h, 32 + side)
        zi, first = ((zp, 0), (zm, SIDES[0]))[side]
        came = rvq[h, first : first + SIDES[side]]
        plus(pv, h, rows(xn, zi, MAIN + first, SIDES[side]), came)
        send(h, 24 + side)

    def value_half(h):
        arrive(h, 23)
        plus(pv, h, rows(x, z2, 0, MAIN), rvx[h, 0, :MAIN])
        send(h, 27)

    def key_side(h, side):
        arrive(h, 16 + side)
        plus(pk, h, (rows(x, zp), rows(xn, zm))[side], rk[h, side])
        send(h, 20 + side)

    def value_block(h, side):
        arrive(h, 24 + side, 27 + side)
        zi = (zp, zm)[side]
        both, alone = ((0, MAIN), (MAIN, REST))[:: 1 - 2 * side]
        for (first, count), twice in ((both, True), (alone, False)):
            came = [rvx[h, 1 + side, first : first + count]]
            if twice:
                came.append(rvh[h, first : first + count])
            plus(pv, h, rows(x, zi, first, count), *came)
        send(h, 29 + side)

    def key_across(h):
        arrive(h, 18, 21)
        plus(pk, h, rows(xn, z), rk[h, 2], rk[h, 5])
        send(h, 22)

    def value_out(h):
        arrive(h, 26, 29, 30)
        dvr_out[:, head_cols(h)] = (
            f32(pv[h, rows(x, z), :]) + f32(rvx[h, 3]) + f32(rvf[h, 0]) + f32(rvf[h, 1])
        ).astype(BF16)

    def key_out(h):
        arrive(h, 19, 20, 22)
        dkr_out[:, head_cols(h)] = (
            f32(pk[h, rows(x, z), :]) + f32(rk[h, 3]) + f32(rk[h, 4]) + f32(rkx[h])
        ).astype(BF16)

    steps = [
        lambda h: send(h, 0),
        lambda h: send(h, 8, 9),
        lambda h: send(h, 7),
        lambda h: send(h, 1, 2),
        lambda h: pass_on(h, (0,), (3, 4)),
        lambda h: pass_on(h, (8,), (12, 10)),
        lambda h: pass_on(h, (9,), (13, 11)),
        lambda h: pass_on(h, (1,), (5,)),
        lambda h: pass_on(h, (4,), (6,)),
        lambda h: pass_on(h, (10,), (14,)),
        lambda h: pass_on(h, (12,), (15,)),
        lambda h: pass_on(h, (13,), (31,)),
        lambda h: value_side(h, 0),
        lambda h: value_side(h, 1),
        value_half,
        lambda h: key_side(h, 0),
        lambda h: key_side(h, 1),
        lambda h: value_block(h, 0),
        lambda h: value_block(h, 1),
        key_across,
        value_out,
        key_out,
        lambda h: late(),
    ]

    def late():
        back = (*range(16, 31), 32, 33)
        for h in range(KVH):
            sent(h, *(slot for slot in back if h < KVH - 1 or slot not in (22, 29, 30)))

    def run(piece, head):
        for number, h in PLAN.get((piece, head), ()):
            steps[number](h)

    def run_when(piece, head, guard=None):
        for h in range(KVH):
            if (piece, h) in PLAN:

                @pl.when(head == h if guard is None else (head == h) & guard)
                def _():
                    run(piece, h)

    barrier = pltpu.get_barrier_semaphore()
    for peer in (right, left, across):
        pl.semaphore_signal(
            barrier, inc=1, device_id={"mem": peer}, device_id_type=pl.DeviceIdType.MESH
        )
    pl.semaphore_wait(barrier, 3)
    for number, h in PLAN[START, 0]:
        if number < FORWARD:
            steps[number](h)
    small = [
        pltpu.make_async_copy(src, dst, isem.at[i])
        for i, (src, dst) in enumerate(
            ((len_hbm, len_in), (fork_hbm, fork_in), (kb_hbm, kb_in), (vb_hbm, vb_in))
        )
    ]
    for one in small:
        one.start()
    for h in range(KVH):
        for which in range(4):
            local(h, which).start()
    for one in small:
        one.wait()

    lens = [len_in[0, b] for b in range(4)]
    ends = [lens[0], lens[0] + lens[1], lens[0] + lens[1] + lens[2]]
    place = lax.broadcasted_iota(jnp.int32, (1, NQ), 1) % TOK
    fork = jnp.full((1, NQ), fork_in[0, 0], jnp.int32)
    start = jnp.zeros((1, NQ), jnp.int32)
    for b, end in enumerate(ends):
        fork = jnp.where(place >= end, fork_in[0, b + 1], fork)
        start = jnp.where(place >= end, end, start)
    fork_row[...] = fork
    start_row[...] = start

    def lay_out(h):
        local(h, 2).wait()
        local(h, 3).wait()
        for g in range(GROUP):
            cols = pl.ds(pl.multiple_of((h * GROUP + g) * HD, HD), HD)
            qs[h, g * TOK : (g + 1) * TOK, :] = q_vm[:, cols]
            gs[h, g * TOK : (g + 1) * TOK, :] = do_vm[:, cols]

    lay_out(0)
    for h in range(KVH):
        local(h, 0).wait()
        local(h, 1).wait()
    for number, h in PLAN[START, 0]:
        if number >= FORWARD:
            steps[number](h)

    order = [
        (x, z), (xn, z), (x, zp), (x, zm), (xn, zp), (xn, zm), (x, z2), (xn, z2),
    ]

    def scores(key, h, lanes):
        return lax.dot_general(key, qs[h, lanes, :], NT, preferred_element_type=F32)

    def grads(value, h, lanes):
        return lax.dot_general(value, gs[h, lanes, :], NT, preferred_element_type=F32)

    lane_tiles = [slice(t, t + LT) for t in range(0, NQ, LT)]

    def first_own(h, par):
        key, value = kb_in[:, head_cols(h)], vb_in[:, head_cols(h)]
        for lanes in lane_tiles:
            row = lax.broadcasted_iota(jnp.int32, (TOK, LT), 0)
            lane = lax.broadcasted_iota(jnp.int32, (TOK, LT), 1) % TOK
            seen = (row <= lane) & (row >= start_row[:, lanes])
            s = jnp.where(seen, scores(key, h, lanes), NEG)
            top = jnp.max(s, axis=0, keepdims=True)
            e = jnp.exp2(s * C2 - top * C2)
            dp = grads(value, h, lanes)
            total[par, :, lanes] = jnp.sum(e, axis=0, keepdims=True)
            corr[par, :, lanes] = jnp.sum(e * dp, axis=0, keepdims=True)
            exp_own[par, :, lanes] = e
            dp_own[par, :, lanes] = dp
            maxes[par, 0:1, lanes] = top

    def first_root(h, par, i, shard):
        here = pl.ds(pl.multiple_of(shard * SHARD, SHARD), SHARD)
        key, value = kbuf[h, here, :], vbuf[h, here, :]
        base = shard * SHARD
        for lanes in lane_tiles:
            row = lax.broadcasted_iota(jnp.int32, (SHARD, LT), 0)
            s = jnp.where(row < fork_row[:, lanes] - base, scores(key, h, lanes), NEG)
            before = maxes[par, pl.ds(i, 1), lanes]
            top = jnp.maximum(before, jnp.max(s, axis=0, keepdims=True))
            shrink = jnp.exp2((before - top) * C2)
            e = jnp.exp2(s * C2 - top * C2)
            dp = grads(value, h, lanes)
            total[par, :, lanes] = total[par, :, lanes] * shrink + jnp.sum(e, axis=0, keepdims=True)
            corr[par, :, lanes] = corr[par, :, lanes] * shrink + jnp.sum(e * dp, axis=0, keepdims=True)
            exp_all[par, i, :, lanes] = e
            dp_all[par, i, :, lanes] = dp
            maxes[par, pl.ds(i + 1, 1), lanes] = top

    def second(h, par, key, e_ref, dp_ref, i):
        turned = key.T
        count = key.shape[0]
        dk = jnp.zeros((count, HD), F32)
        dv = jnp.zeros((count, HD), F32)
        for lanes in lane_tiles:
            p = e_ref[:, lanes] * maxes[par, pl.ds(i, 1), lanes]
            ds = (p * (dp_ref[:, lanes] - corr[par, :, lanes])).astype(BF16)
            dk += jnp.dot(ds, qs[h, lanes, :], preferred_element_type=F32)
            dv += jnp.dot(p.astype(BF16), gs[h, lanes, :], preferred_element_type=F32)
            dq_acc[:, lanes] += jnp.dot(turned, ds, preferred_element_type=F32)
        return (dk * SCALE).astype(BF16), dv.astype(BF16)

    def second_root(h, par, i, shard):
        here = pl.ds(pl.multiple_of(shard * SHARD, SHARD), SHARD)
        dk, dv = second(h, par, kbuf[h, here, :], exp_all.at[par, i], dp_all.at[par, i], i + 1)
        pk[h, here, :] = dk
        pv[h, here, :] = dv

    def when(condition, step, *args):
        @pl.when(condition)
        def _():
            step(*args)

    shards = [at(xi, zi) for xi, zi in order]

    def step(s, carry):
        now, after = s - 1, s
        odd = s % 2
        even = 1 - odd

        @pl.when(s < KVH)
        def _():
            first_own(after, odd)

        @pl.when(s < KVH - 1)
        def _():
            lay_out(s + 1)

        run_when(OWN, s)

        def first_group(far, carry):
            h = s - far
            par = (odd + far) % 2
            when(far == 0, arrive, h, 7)
            when(far == 1, arrive, h, 3)
            for c in range(4):
                if c == 2:

                    run_when(NEAR_A, h, far == 0)
                    run_when(FAR_A, h, far == 1)
                    when(far == 0, arrive, h, 2)
                    when(far == 1, arrive, h, 5, 11, 6, 14, 15, 31)
                first_root(h, par, far * 4 + c, jnp.where(far == 0, shards[c], shards[4 + c]))
            run_when(NEAR_B, h, far == 0)
            run_when(FAR_B, h, far == 1)
            return carry

        lax.fori_loop(jnp.where(s == KVH, 1, 0), jnp.where(s == 0, 1, 2), first_group, 0)

        def second_half():
            h = now
            inverse = 1.0 / total[even]
            maxes[even] = jnp.exp2((maxes[even] - maxes[even, N_MEM : N_MEM + 1, :]) * C2) * inverse
            corr[even] = corr[even] * inverse
            dq_acc[...] = jnp.zeros((HD, NQ), F32)

            def second_group(near, carry):
                for c, (i, j) in enumerate(((7, 2), (6, 3), (4, 1), (5, 0))):
                    second_root(
                        h, even, jnp.where(near == 0, i, j),
                        jnp.where(near == 0, shards[i], shards[j]),
                    )
                    if c == 1:
                        when(near == 0, send, h, 23, 17, 16, 32, 33, 28)
                        when(near == 1, send, h, 19)

                        run_when(BACK_A, h, near == 0)
                        run_when(BACK_C, h, near == 1)
                when(near == 0, send, h, 18)
                when(near == 1, send, h, 26)
                run_when(BACK_B, h, near == 0)
                run_when(BACK_D, h, near == 1)
                return carry

            lax.fori_loop(0, 2, second_group, 0)
            dk, dv = second(h, even, kb_in[:, head_cols(h)], exp_own.at[even], dp_own.at[even], 0)
            dkb_out[:, head_cols(h)] = dk
            dvb_out[:, head_cols(h)] = dv
            for g in range(GROUP):
                cols = pl.ds(pl.multiple_of((h * GROUP + g) * HD, HD), HD)
                dq_out[:, cols] = (dq_acc[:, g * TOK : (g + 1) * TOK].T * SCALE).astype(BF16)
            sent(h, *range(16), 31)
            run_when(DONE, h)

        when(s > 0, second_half)
        return carry

    lax.fori_loop(0, KVH + 1, step, 0)

    sent(KVH - 1, 22, 29, 30)


def hand_over(dq, dkb, dvb, dkr, dvr, dq_out, dkb_out, dvb_out, dkr_out, dvr_out, gone):
    srcs, dsts = (dq, dkb, dvb, dkr, dvr), (dq_out, dkb_out, dvb_out, dkr_out, dvr_out)
    outs = []
    for src, dst in zip(srcs, dsts):
        parts = max(1, src.size // (SHARD * KVH * HD))
        count = src.shape[0] // parts
        for part in range(parts):
            here = pl.ds(part * count, count)
            outs.append(pltpu.make_async_copy(src.at[here], dst.at[here], gone.at[len(outs)]))
    for one in outs:
        one.start()
    for one in outs:
        one.wait()


def per_device(*args):
    vmem, anywhere = (pl.BlockSpec(memory_space=space) for space in (pltpu.VMEM, pl.ANY))
    buf = pltpu.VMEM
    outs = pl.pallas_call(
        kernel,
        out_shape=(
            buf((TOK, KVH * GROUP * HD), BF16),
            buf((TOK, KVH * HD), BF16),
            buf((TOK, KVH * HD), BF16),
            buf((SHARD, KVH * HD), BF16),
            buf((SHARD, KVH * HD), BF16),
        ),
        in_specs=[anywhere] * 8,
        out_specs=(vmem,) * 5,
        scratch_shapes=[
            buf((TOK, KVH * NQ), BF16),
            buf((TOK, KVH * NQ), BF16),
            buf((TOK, KVH * HD), BF16),
            buf((TOK, KVH * HD), BF16),
            pltpu.SMEM((1, 4), jnp.int32),
            pltpu.SMEM((1, 4), jnp.int32),
            buf((KVH, NQ, HD), BF16),
            buf((KVH, NQ, HD), BF16),
            buf((KVH, ROOT, HD), BF16),
            buf((KVH, ROOT, HD), BF16),
            buf((KVH, ROOT, HD), BF16),
            buf((KVH, ROOT, HD), BF16),
            buf((KVH, 6, SHARD, HD), BF16),
            buf((KVH, SHARD, HD), BF16),
            buf((KVH, 4, SHARD, HD), BF16),
            buf((KVH, SHARD, HD), BF16),
            buf((KVH, 2, SHARD, HD), BF16),
            buf((KVH, REST, HD), BF16),
            buf((2, TOK, NQ), F32),
            buf((2, TOK, NQ), F32),
            buf((2, N_MEM, SHARD, NQ), F32),
            buf((2, N_MEM, SHARD, NQ), F32),
            buf((2, N_MEM + 1, NQ), F32),
            buf((2, 1, NQ), F32),
            buf((2, 1, NQ), F32),
            buf((HD, NQ), F32),
            buf((1, NQ), jnp.int32),
            buf((1, NQ), jnp.int32),
            pltpu.SemaphoreType.DMA((KVH, SLOTS)),
            pltpu.SemaphoreType.DMA((KVH, SLOTS)),
            pltpu.SemaphoreType.DMA((KVH, 4)),
            pltpu.SemaphoreType.DMA((4,)),
        ],
        compiler_params=pltpu.CompilerParams(
            collective_id=0, has_side_effects=True, vmem_limit_bytes=60 * 2**20
        ),
        cost_estimate=pl.CostEstimate(
            flops=12 * 10**9, bytes_accessed=6 * 10**6, transcendentals=9 * 10**6
        ),
    )(*args)
    return pl.pallas_call(
        hand_over,
        out_shape=tuple(jax.ShapeDtypeStruct(out.shape, out.dtype) for out in outs),
        in_specs=[anywhere] * 5,
        out_specs=(anywhere,) * 5,
        scratch_shapes=[pltpu.SemaphoreType.DMA((8,))],
    )(*[pltpu.with_memory_space_constraint(out, pltpu.VMEM) for out in outs])


def solution(mesh):
    spec = P(("grp", "mem"), None)
    return jax.shard_map(
        per_device,
        mesh=mesh,
        in_specs=(spec,) * 8,
        out_specs=(spec,) * 5,
        check_vma=False,
    )
```
